512 devices in a mesh: wide: 64 (over y, z_lo, core), narrow: 8 (over z_hi, x).
Axes of the slice: x: 4, y: 4, z: 16 (z_hi: 2, z_lo: 8; z = z_hi * 8 + z_lo), core: 2. Of those that a mesh axis runs over, the one named last changes fastest.
Arguments:
- spin: float32 [3, 32, 128, 1024], P(None, None, 'wide', 'narrow'), may hold values from -1 to 1, as said below
- region: int32 [32, 128, 1024], P(None, 'wide', 'narrow'), may hold values 0 or 1
- material: int32 [32, 128, 1024], P(None, 'wide', 'narrow'), may hold values from 0 to 3
- saturation: float32 [4], replicated, may hold values from 0.5 to 2
- anisotropy: float32 [4], replicated, may hold values from 0.2 to 1
- damping: float32 [4], replicated, may hold values from 0.05 to 0.5
- applied: float32 [3], replicated, may hold values from -3 to 3
- demag_spectrum: bfloat16 [6, 64, 256, 2048], P(None, 'wide', 'narrow'), may hold values from -2.5 to 2.5, as said below
Outputs:
- rate: float32 [3, 32, 128, 1024], P(None, None, 'wide', 'narrow')
- demag_field: float32 [3, 32, 128, 1024], P(None, None, 'wide', 'narrow')
The draws below stay inside these ranges and needn't reach their ends.
Inputs may be any that keep to these rules, and one draw needn't show every extreme that they name: `spin`: every cell's three components form a unit vector. `demag_spectrum`: every component is unchanged when all three wave numbers are replaced by their negatives modulo 64, 256, 2048.
All inputs are finite; a program needn't handle non-finite values. No bound on the sum of `region` on one device may be relied on, other than what follows from the above.
Results may differ from the reference program's by a relative error of at most 0.0003.
Values sent between devices are 32-bit elements; how exact they have to be, the bound alone decides.
A program may use at most 64 MiB of HBM per device.

```python
import math
import jax
import jax.numpy as jnp

NZ = 32
MATERIALS = 4
NX = 128
NY = 1024
LZ = 64
LX = 256
LY = 2048


def draw_spin(key, part):
    first, second = jax.random.split(jax.random.fold_in(key, 11))
    height = jax.random.uniform(first, (NZ, NX, NY), jnp.float32, -1.0, 1.0)
    azimuth = jax.random.uniform(second, (NZ, NX, NY), jnp.float32, -math.pi, math.pi)
    radius = jnp.sqrt(jnp.maximum(1.0 - height * height, 0.0))
    return jnp.stack([radius * jnp.cos(azimuth), radius * jnp.sin(azimuth), height])


def mirror(values):
    return jnp.roll(jnp.flip(values, axis=(1, 2, 3)), (1, 1, 1), axis=(1, 2, 3))


def symbols(length):
    phase = jnp.arange(length).astype(jnp.float32) * (math.pi / length)
    return (2.0 * jnp.sin(2.0 * phase), 4.0 * jnp.sin(phase) * jnp.sin(phase))


def draw_demag_spectrum(key, part):
    first, second = jax.random.split(jax.random.fold_in(key, 23))
    odd_z, square_z = symbols(LZ)
    odd_x, square_x = symbols(LX)
    odd_y, square_y = symbols(LY)
    odd_z, square_z = (odd_z[:, None, None], square_z[:, None, None])
    odd_x, square_x = (odd_x[None, :, None], square_x[None, :, None])
    odd_y, square_y = (odd_y[None, None, :], square_y[None, None, :])
    denominator = square_x + square_y + square_z + 0.1
    base = jnp.stack([square_x + 0.0 * odd_y + 0.0 * odd_z, square_y + 0.0 * odd_x + 0.0 * odd_z, square_z + 0.0 * odd_x + 0.0 * odd_y, odd_x * odd_y + 0.0 * odd_z, odd_x * odd_z + 0.0 * odd_y, odd_y * odd_z + 0.0 * odd_x]) / denominator[None]
    gains = jax.random.uniform(first, (6, LZ, LX, LY), jnp.float32, 0.6, 1.4)
    noise = jax.random.uniform(second, (6, LZ, LX, LY), jnp.float32, -0.3, 0.3)
    values = base * gains + noise
    return jnp.clip(0.5 * (values + mirror(values)), -2.5, 2.5).astype(jnp.bfloat16)


def plant(values, key, low, largest):
    longest = values.shape.index(max(values.shape))
    spots = []
    for shift in (0, 1):
        where = [jax.random.randint(jax.random.fold_in(key, axis), (), 0, length) for axis, length in enumerate(values.shape)]
        where[longest] = (where[longest] + shift) % values.shape[longest]
        spots.append(tuple(where))
    return values.at[spots[0]].set(low).at[spots[1]].set(largest)


def scatter_about(stream_key, shape, width, most, kind=jnp.bfloat16):
    return jnp.clip(width * jax.random.normal(stream_key, shape, jnp.float32), -most, most).astype(kind)


def setup_inputs(seed: int = 0) -> dict:
    key_of = jax.random.split(jax.random.key(seed), 9)
    spin = draw_spin(jax.random.fold_in(key_of[8], 71), 0)
    region = plant((jax.random.randint(key_of[1], (NZ, NX, NY), 0, 8) < 7).astype(jnp.int32), jax.random.fold_in(key_of[1], 1), 0, 1)
    material = plant(jax.random.randint(key_of[2], (NZ, NX, NY), 0, MATERIALS), jax.random.fold_in(key_of[2], 1), 0, MATERIALS - 1).astype(jnp.int32)
    saturation = jnp.clip(jnp.exp(jax.random.uniform(key_of[3], (MATERIALS,), jnp.float32, math.log(0.5), math.log(2.0))), 0.5, 2.0)
    anisotropy = jnp.clip(jnp.exp(jax.random.uniform(key_of[4], (MATERIALS,), jnp.float32, math.log(0.2), math.log(1.0))), 0.2, 1.0)
    damping = jnp.clip(jnp.exp(jax.random.uniform(key_of[5], (MATERIALS,), jnp.float32, math.log(0.05), math.log(0.5))), 0.05, 0.5)
    applied = scatter_about(key_of[6], (3,), 1.0, 3.0, jnp.float32)
    demag_spectrum = draw_demag_spectrum(jax.random.fold_in(key_of[8], 71), 0)
    return dict(spin=spin, region=region, material=material, saturation=saturation, anisotropy=anisotropy, damping=damping, applied=applied, demag_spectrum=demag_spectrum)


exchange_coef = 0.3


def cross(left, right):
    return jnp.stack([left[1] * right[2] - left[2] * right[1],
                      left[2] * right[0] - left[0] * right[2],
                      left[0] * right[1] - left[1] * right[0]])


def reference(spin, region, material, saturation, anisotropy, damping, applied, demag_spectrum):
    magnet = region.astype(jnp.float32)
    direction = spin * magnet[None]
    sat_cell = saturation[material]
    anis_cell = anisotropy[material]
    damp_cell = damping[material]
    moment = direction * sat_cell[None]
    padded = jnp.pad(moment, ((0, 0), (0, NZ), (0, NX), (0, NY)))
    spectrum = jnp.fft.rfftn(padded, axes=(1, 2, 3))
    kernel = demag_spectrum.astype(jnp.float32)[:, :, :, :NY + 1]
    couplings = ((0, 3, 4), (3, 1, 5), (4, 5, 2))
    pieces = []
    for picks in couplings:
        mixed = kernel[picks[0]] * spectrum[0] + kernel[picks[1]] * spectrum[1] + kernel[picks[2]] * spectrum[2]
        inverse = jnp.fft.irfftn(mixed, s=(LZ, LX, LY), axes=(0, 1, 2))
        pieces.append(-inverse[:NZ, :NX, :NY])
    demag = jnp.stack(pieces)
    framed = jnp.pad(direction, ((0, 0), (1, 1), (1, 1), (1, 1)))
    weight = jnp.sum(framed * framed, axis=0)
    neighbours = (framed[:, 2:, 1:-1, 1:-1] + framed[:, :-2, 1:-1, 1:-1]
                  + framed[:, 1:-1, 2:, 1:-1] + framed[:, 1:-1, :-2, 1:-1]
                  + framed[:, 1:-1, 1:-1, 2:] + framed[:, 1:-1, 1:-1, :-2])
    present = (weight[2:, 1:-1, 1:-1] + weight[:-2, 1:-1, 1:-1]
               + weight[1:-1, 2:, 1:-1] + weight[1:-1, :-2, 1:-1]
               + weight[1:-1, 1:-1, 2:] + weight[1:-1, 1:-1, :-2])
    laplace = neighbours - present[None] * direction
    zeros = jnp.zeros_like(sat_cell)
    uniaxial = jnp.stack([zeros, zeros, 2.0 * anis_cell / sat_cell * direction[2]])
    field = exchange_coef * laplace / sat_cell[None] + demag + applied[:, None, None, None] + uniaxial
    torque = cross(direction, field)
    rate = -(torque + damp_cell[None] * cross(direction, torque)) / (1.0 + damp_cell * damp_cell)[None]
    return rate, demag
```

```python
import functools
import math

import jax
import jax.numpy as jnp
import ml_dtypes
import numpy as np
from jax import lax
from jax.experimental import pallas as pl
from jax.experimental.pallas import tpu as pltpu
from jax.sharding import PartitionSpec as P

EXCHANGE = 0.3
MESH = pl.DeviceIdType.MESH
WIDE, NARROW = 64, 8
NZ, LZ, NX, LX, NY, LY = 32, 64, 128, 256, 1024, 2048
ROWS = 16
GROUP = 2 * NARROW
LANES = 128
HALF = 64
MSG = 6 * LANES
F32, BF16 = jnp.float32, jnp.bfloat16


def halves(x):
    hi = x.astype(np.float32).astype(ml_dtypes.bfloat16)
    lo = (x - hi.astype(np.float64)).astype(ml_dtypes.bfloat16)
    return hi, lo


def slots():
    row = np.arange(WIDE)
    return np.where(row <= 32, row % 32, WIDE - row)


def z_forward():
    s, z = slots()[:, None], np.arange(NZ)[None]
    angle = 2 * np.pi * (s * z % LZ) / LZ
    re = np.cos(angle)
    im = np.where(s == 0, np.where(z % 2, -1.0, 1.0), -np.sin(angle))
    return np.concatenate([re, im], 0)


def z_inverse():
    parts = z_forward().reshape(2, 2, 32, NZ)
    return parts.transpose(3, 1, 0, 2).reshape(NZ, 128)


def x_order():
    return np.arange(NX).reshape(WIDE, 2).T.reshape(-1)


def kx_rows():
    start = 32 * np.arange(NARROW)[:, None]
    return np.concatenate([(start + np.arange(ROWS)[None]).reshape(-1), start[:, 0] + ROWS])


def x_forward():
    kx = kx_rows()
    angle = 2 * np.pi * (kx[:, None] * x_order()[None] % LX) / LX
    return np.concatenate([np.cos(angle), -np.sin(angle)], 1)


def x_inverse():
    kx = kx_rows()
    weight = np.where(kx % 16 == 0, 1.0, 2.0) / (LZ * LX * LY)
    angle = 2 * np.pi * (x_order()[:, None] * kx[None] % LX) / LX
    return np.concatenate([np.cos(angle) * weight, np.sin(angle) * weight], 1)


def y_inner(sign):
    p = np.arange(HALF)
    angle = sign * 2 * np.pi * (p[:, None] * p[None] % HALF) / HALF
    c, s = np.cos(angle), np.sin(angle)
    return np.block([[c, s], [-s, c]])


def y_twist():
    k, p = np.arange(32)[:, None], np.arange(HALF)[None]
    angle = -2 * np.pi * (k * p) / LY
    c, s = np.cos(angle), np.sin(angle)
    both = np.stack([np.concatenate([c, c], 1), np.concatenate([-s, s], 1)])
    return both.astype(np.float32)


DIAGONALS = ((0, 1, 2), (3, 5, 4), (4, 3, 5))
ROWS_OF = ((0, 3, 4), (3, 1, 5), (4, 5, 2))


def mm(a, b):
    dot = functools.partial(jnp.dot, preferred_element_type=F32)
    return dot(a[0], b[0]) + (dot(a[0], b[1]) + dot(a[1], b[0]))


def split(x):
    hi = x.astype(BF16)
    return hi, (x - hi.astype(F32)).astype(BF16)


def tiles(x):
    return [x[:, i:i + LANES] for i in range(0, x.shape[1], LANES)]


def swap(x):
    return jnp.concatenate([pltpu.roll(t, HALF, 1) for t in tiles(x)], 1)


def low_half(shape):
    return (lax.broadcasted_iota(jnp.int32, shape, 1) & (LANES - 1)) < HALF


def sign_of(shape):
    return jnp.where(low_half(shape), -1.0, 1.0).astype(F32)


def turn(v, angle, sign):
    c, s = math.cos(angle), math.sin(angle)
    if abs(s) < 1e-9 and c > 0:
        return v
    j = pltpu.roll(v, HALF, 1) * sign
    if abs(c) < 1e-9:
        return j if s > 0 else -j
    if abs(c - s) < 1e-9:
        return (v + j) * c
    if abs(c + s) < 1e-9:
        return (v - j) * c
    return v * c + j * s


def fft(values, direction, sign):
    n = len(values)
    if n == 1:
        return values
    even = fft(values[0::2], direction, sign)
    odd = fft(values[1::2], direction, sign)
    odd = [turn(o, direction * 2 * math.pi * k / n, sign) for k, o in enumerate(odd)]
    return [e + o for e, o in zip(even, odd)] + [e - o for e, o in zip(even, odd)]


def shifted(x, step):
    zero = jnp.zeros((1, x.shape[1]), x.dtype)
    if step > 0:
        return jnp.concatenate([x[1:], zero], 0)
    return jnp.concatenate([zero, x[:-1]], 0)


def kernel(spin, region, material, satur, aniso, damp, applied, demag_spec,
           zf_hi, zf_lo, zi_hi, zi_lo, xf_hi, xf_lo, xi_hi, xi_lo,
           wf_hi, wf_lo, wi_hi, wi_lo, twist,
           rate_out, demag_out,
           s1, r1, s2, r2, s3, r3, s4, r4, s2e, r2e, s3e, r3e, spare, tensor, tensor_e, work, base,
           hx_send, hx, hy_send, hy, send, recv, hsend, hrecv):
    w, n = lax.axis_index("wide"), lax.axis_index("narrow")
    upper = jnp.where(w >= 32, 1, 0)
    mate = jnp.where(lax.rem(w, 32) == 0, 32 - w, WIDE - w)
    row_low = jnp.where(upper == 1, mate, w)
    row_high = jnp.where(upper == 1, w, mate)
    special = lax.rem(w, 32) == 0
    me = upper * NARROW + n

    def pair_device(t):
        return (jnp.where(t >= NARROW, row_high, row_low), lax.rem(t, NARROW))

    barrier = pltpu.get_barrier_semaphore()

    def greet_wide(i, carry):
        pl.semaphore_signal(barrier, inc=1, device_id=(lax.rem(w + i, WIDE), n), device_id_type=MESH)
        return carry

    def greet_pair(i, carry):
        pl.semaphore_signal(barrier, inc=1, device_id=pair_device(lax.rem(me + i, GROUP)), device_id_type=MESH)
        return carry

    lax.fori_loop(1, WIDE, greet_wide, 0)
    lax.fori_loop(1, GROUP, greet_pair, 0)

    direction = {}
    sat = {}
    for xx in range(2):
        rows = pl.ds(xx, NZ, stride=2)
        mag = region[rows, :].astype(F32)
        mat = material[rows, :]

        def lookup(table):
            out = jnp.full(mat.shape, table[3], F32)
            for i in range(3):
                out = jnp.where(mat == i, table[i], out)
            return out

        sat[xx] = lookup(satur)
        for c in range(3):
            direction[c, xx] = spin[c, rows, :] * mag
    moment = jnp.concatenate([direction[c, xx] * sat[xx] for xx in range(2) for c in range(3)], 1)
    spec = mm((zf_hi[...], zf_lo[...]), split(moment))
    re, im = spec[:WIDE], spec[WIDE:]
    left = low_half((32, MSG))
    s1[0:32, :] = jnp.where(left, re[:32], swap(im[:32]))
    s1[32:64, :] = jnp.where(left, swap(re[32:]), im[32:])

    lane = lax.broadcasted_iota(jnp.int32, (NZ, LANES), 1)
    for xx in range(2):
        for c in range(3):
            hx_send[1 - xx, NZ * c:NZ * c + NZ, :] = direction[c, xx]
        for side, at in ((0, LANES - 1), (1, 0)):
            cols = [jnp.broadcast_to(direction[c, xx][:, at:at + 1], (NZ, LANES)) for c in range(3)]
            hy_send[side, NZ * xx:NZ * xx + NZ, :] = jnp.where(
                lane == 0, cols[0], jnp.where(lane == 1, cols[1], cols[2]))

    pl.semaphore_wait(barrier, WIDE - 1 + GROUP - 1)

    def local(src, dst, sem):
        return pltpu.make_async_copy(src, dst, sem)

    def rows_start(src, dst, i, mine, count, device):
        def go(step, carry):
            t = lax.rem(mine + step, count)
            pltpu.make_async_remote_copy(
                src.at[pl.ds(t, 1)], dst.at[pl.ds(mine, 1)], send.at[i], recv.at[i],
                device_id=device(t), device_id_type=MESH).start()
            return carry
        lax.fori_loop(1, count, go, 0)
        own = src.at[pl.ds(mine, 1)]
        local(own, dst.at[pl.ds(mine, 1)], recv.at[i]).start()
        local(own, spare.at[pl.ds(0, 1), pl.ds(0, src.shape[1])], send.at[i]).start()

    def wide_device(t):
        return (t, n)

    def blocks_start(src, dst, i):
        def go(step, carry):
            t = lax.rem(me + step, GROUP)
            pltpu.make_async_remote_copy(
                src.at[t], dst.at[me], send.at[i], recv.at[i],
                device_id=pair_device(t), device_id_type=MESH).start()
            return carry
        lax.fori_loop(1, GROUP, go, 0)
        local(src.at[me], dst.at[me], recv.at[i]).start()

    def rows_wait(src, dst, i):
        local(dst, dst, recv.at[i]).wait()
        local(src, src, send.at[i]).wait()

    def blocks_wait(src, dst, i):
        local(dst, dst, recv.at[i]).wait()
        part = src.at[pl.ds(0, GROUP - 1)]
        local(part, part, send.at[i]).wait()

    halo = []
    for side, step in ((0, 1), (1, WIDE - 1)):
        halo.append(pltpu.make_async_remote_copy(
            hx_send.at[side], hx.at[side], hsend.at[side], hrecv.at[side],
            device_id=(lax.rem(w + step, WIDE), n), device_id_type=MESH))
    for side, step in ((0, 1), (1, NARROW - 1)):
        halo.append(pltpu.make_async_remote_copy(
            hy_send.at[side], hy.at[side], hsend.at[2 + side], hrecv.at[2 + side],
            device_id=(w, lax.rem(n + step, NARROW)), device_id_type=MESH))

    rows_start(s1, r1, 0, w, WIDE, wide_device)
    for copy in halo:
        copy.start()

    flat = demag_spec[...].reshape(6 * 32, LY)

    def reorder(q, carry):
        ky = lax.broadcasted_iota(jnp.int32, (LY, LANES), 0)
        col = lax.broadcasted_iota(jnp.int32, (LY, LANES), 1)
        target = 32 * (col & (HALF - 1)) + 2 * q + lax.shift_right_logical(col, 6)
        pick = jnp.where(ky == target, 1.0, 0.0).astype(BF16)
        got = jnp.dot(flat, pick, preferred_element_type=F32)
        other = pltpu.roll(got, HALF, 1)
        left = low_half(got.shape)
        for half, both in ((0, jnp.where(left, got, other)), (1, jnp.where(left, other, got))):
            at = pl.multiple_of(16 * q + 8 * half, 8)
            for g in range(6):
                for t in range(2):
                    tensor[t, g, pl.ds(at, 8), :] = both[32 * g + 8 * t:32 * g + 8 * t + 8]
            for d in range(3):
                extra = [both[32 * g + ROWS:32 * g + ROWS + 1] for g in DIAGONALS[d]]
                tensor_e[d, pl.ds(at, 8), :] = jnp.concatenate(extra + [jnp.zeros((5, LANES), F32)], 0)
        return carry

    lax.fori_loop(0, 16, reorder, 0)

    rows_wait(s1, r1, 0)
    got = r1[...]
    z = jnp.concatenate([got[:, :3 * LANES], got[:, 3 * LANES:]], 0)
    left = low_half(z.shape)
    sign = sign_of(z.shape)
    zero = jnp.zeros_like(z)
    z_swap = swap(z)
    low = jnp.where(special, jnp.where(left, z, zero), z)
    high = jnp.where(special, jnp.where(left, z_swap, zero), z * (-sign))
    rhs = jnp.concatenate([
        jnp.concatenate([low, high], 1),
        jnp.concatenate([swap(low) * sign, swap(high) * sign], 1)], 0)
    out = mm((xf_hi[...], xf_lo[...]), split(rhs))
    for q in range(2):
        part = out[:, 3 * LANES * q:3 * LANES * (q + 1)]
        for b in range(NARROW):
            s2[q * NARROW + b] = part[ROWS * b:ROWS * b + ROWS]
        s2e[q * NARROW:q * NARROW + NARROW, :] = part[NARROW * ROWS:]
    blocks_start(s2, r2, 1)
    rows_start(s2e, r2e, 2, me, GROUP, pair_device)

    for copy in halo:
        copy.wait()
    inside = [jnp.where(w > 0, 1.0, 0.0), jnp.where(w < WIDE - 1, 1.0, 0.0),
              jnp.where(n > 0, 1.0, 0.0), jnp.where(n < NARROW - 1, 1.0, 0.0)]
    for xx in range(2):
        total = [jnp.zeros((NZ, LANES), F32)] * 3
        weight = jnp.zeros((NZ, LANES), F32)
        here = [direction[c, xx] for c in range(3)]

        def x_halo(side):
            return [hx[side, NZ * c:NZ * c + NZ, :] * inside[side] for c in range(3)]

        def y_edge(side, c):
            column = hy[side, NZ * xx:NZ * xx + NZ, c:c + 1] * inside[2 + side]
            return jnp.broadcast_to(column, (NZ, LANES))

        neighbours = [
            [shifted(d, 1) for d in here],
            [shifted(d, -1) for d in here],
            [direction[c, 0] for c in range(3)] if xx == 1 else x_halo(0),
            [direction[c, 1] for c in range(3)] if xx == 0 else x_halo(1),
            [jnp.where(lane == LANES - 1, y_edge(1, c), pltpu.roll(here[c], LANES - 1, 1)) for c in range(3)],
            [jnp.where(lane == 0, y_edge(0, c), pltpu.roll(here[c], 1, 1)) for c in range(3)],
        ]
        for near in neighbours:
            total = [a + b for a, b in zip(total, near)]
            weight = weight + (near[0] * near[0] + near[1] * near[1] + near[2] * near[2])
        mat = material[pl.ds(xx, NZ, stride=2), :]
        anis_cell = jnp.full(mat.shape, aniso[3], F32)
        for i in range(3):
            anis_cell = jnp.where(mat == i, aniso[i], anis_cell)
        for c in range(3):
            part = EXCHANGE * (total[c] - weight * here[c]) / sat[xx] + applied[c]
            if c == 2:
                part = part + 2.0 * anis_cell / sat[xx] * here[2]
            base[c, NZ * xx:NZ * xx + NZ, :] = part

    blocks_wait(s2, r2, 1)
    rows_wait(s2e, r2e, 2)
    sign8 = sign_of((8, LANES))

    def source(b):
        return (b % 2) * NARROW + b // 2

    def y_forward(v):
        even = fft(v, -1, sign8)
        odd = fft([turn(x, -2 * math.pi * b / 32, sign8) for b, x in enumerate(v)], -1, sign8)
        for k in range(32):
            u = even[k // 2] if k % 2 == 0 else odd[k // 2]
            work[8 * k:8 * k + 8, :] = (
                u * twist[0, k:k + 1, :] + pltpu.roll(u, HALF, 1) * twist[1, k:k + 1, :])
        return mm(split(work[...]), (wf_hi[...], wf_lo[...]))

    def y_inverse(field):
        work[...] = mm(split(field), (wi_hi[...], wi_lo[...]))
        u = []
        for k in range(32):
            x = work[8 * k:8 * k + 8, :]
            u.append(x * twist[0, k:k + 1, :] - pltpu.roll(x, HALF, 1) * twist[1, k:k + 1, :])
        even = fft(u[0::2], 1, sign8)
        odd = fft(u[1::2], 1, sign8)
        return [even[b] + turn(odd[b], 2 * math.pi * b / 32, sign8) for b in range(16)]

    def y_block(t, carry):
        rows = pl.ds(pl.multiple_of(8 * t, 8), 8)
        spectra = [
            y_forward([r2[source(b), rows, LANES * c:LANES * c + LANES] for b in range(16)])
            for c in range(3)
        ]
        for c, picks in enumerate(ROWS_OF):
            field = -(tensor[t, picks[0]] * spectra[0] + tensor[t, picks[1]] * spectra[1]
                      + tensor[t, picks[2]] * spectra[2])
            for b, x in enumerate(y_inverse(field)):
                s3[source(b), rows, LANES * c:LANES * c + LANES] = x
        return carry

    lax.fori_loop(0, 2, y_block, 0)
    blocks_start(s3, r3, 3)
    v = []
    for b in range(16):
        row = [r2e[source(b):source(b) + 1, LANES * c:LANES * c + LANES] for c in range(3)]
        v.append(jnp.concatenate(row + row + row[:2], 0))
    spectrum = y_forward(v)
    field = -(tensor_e[0] * spectrum + tensor_e[1] * pltpu.roll(spectrum, 255, 0)
              + tensor_e[2] * pltpu.roll(spectrum, 254, 0))
    for b, x in enumerate(y_inverse(field)):
        for c in range(3):
            s3e[source(b):source(b) + 1, LANES * c:LANES * c + LANES] = x[c:c + 1]
    rows_start(s3e, r3e, 4, me, GROUP, pair_device)
    blocks_wait(s3, r3, 3)
    rows_wait(s3e, r3e, 4)

    got = r3[...].reshape(GROUP * ROWS, 3 * LANES)
    low = jnp.concatenate([got[:NARROW * ROWS], r3e[:NARROW, :]], 0)
    high = jnp.concatenate([got[NARROW * ROWS:], r3e[NARROW:, :]], 0)
    sign = sign_of(low.shape)
    rhs = jnp.concatenate([
        jnp.concatenate([low, high], 1),
        jnp.concatenate([swap(low) * sign, swap(high) * sign], 1)], 0)
    out = mm((xi_hi[...], xi_lo[...]), split(rhs))
    low, high = out[:, :3 * LANES], out[:, 3 * LANES:]
    left = low_half(low.shape)
    sign = sign_of(low.shape)
    slot = jnp.where(special, jnp.where(left, low, swap(high)), low - high * sign)
    s4[:, :3 * LANES] = slot[:WIDE]
    s4[:, 3 * LANES:] = slot[WIDE:]
    rows_start(s4, r4, 5, w, WIDE, wide_device)
    rows_wait(s4, r4, 5)

    got = r4[...]
    first, second = got[:32], got[32:]
    left = low_half(first.shape)
    zero = jnp.zeros_like(first)
    rhs = jnp.concatenate([
        jnp.where(left, first, zero), jnp.where(left, swap(first), zero),
        jnp.where(left, zero, swap(second)), jnp.where(left, zero, second)], 0)
    field = mm((zi_hi[...], zi_lo[...]), split(rhs))
    for xx in range(2):
        rows = pl.ds(xx, NZ, stride=2)
        h = []
        for c in range(3):
            at = LANES * (3 * xx + c)
            h.append(field[:, at:at + LANES])
            demag_out[c, rows, :] = h[c]
        mat = material[rows, :]
        a = jnp.full(mat.shape, damp[3], F32)
        for i in range(3):
            a = jnp.where(mat == i, damp[i], a)
        h = [h[c] + base[c, NZ * xx:NZ * xx + NZ, :] for c in range(3)]
        d = [direction[c, xx] for c in range(3)]

        def cross(x, y):
            return [x[1] * y[2] - x[2] * y[1], x[2] * y[0] - x[0] * y[2], x[0] * y[1] - x[1] * y[0]]

        torque = cross(d, h)
        second_torque = cross(d, torque)
        for c in range(3):
            rate_out[c, rows, :] = -(torque[c] + a * second_torque[c]) / (1.0 + a * a)


def shards(spin, region, material, saturation, anisotropy, damping, applied, demag_spectrum):
    vmem = pl.BlockSpec(memory_space=pltpu.VMEM)
    smem = pl.BlockSpec(memory_space=pltpu.SMEM)
    tables = []
    for table in (z_forward(), z_inverse(), x_forward(), x_inverse(), y_inner(-1), y_inner(1)):
        tables.extend(jnp.asarray(part) for part in halves(table))
    tables.append(jnp.asarray(y_twist()))
    dma = pltpu.SemaphoreType.DMA
    out = jax.ShapeDtypeStruct((3, 2 * NZ, LANES), F32)
    rate, demag = pl.pallas_call(
        kernel,
        out_shape=(out, out),
        in_specs=[vmem] * 3 + [smem] * 4 + [vmem] * (1 + len(tables)),
        out_specs=(vmem, vmem),
        scratch_shapes=[pltpu.VMEM((WIDE, MSG), F32)] * 2
        + [pltpu.VMEM((GROUP, ROWS, 3 * LANES), F32)] * 4
        + [pltpu.VMEM((WIDE, MSG), F32)] * 2
        + [pltpu.VMEM((GROUP, 3 * LANES), F32)] * 4
        + [
            pltpu.VMEM((8, MSG), F32),
            pltpu.VMEM((2, 6, 256, LANES), F32),
            pltpu.VMEM((3, 256, LANES), F32),
            pltpu.VMEM((256, LANES), F32),
            pltpu.VMEM((3, 2 * NZ, LANES), F32),
            pltpu.VMEM((2, 3 * NZ, LANES), F32),
            pltpu.VMEM((2, 3 * NZ, LANES), F32),
            pltpu.VMEM((2, 2 * NZ, LANES), F32),
            pltpu.VMEM((2, 2 * NZ, LANES), F32),
        ]
        + [dma((6,)), dma((6,)), dma((4,)), dma((4,))],
        compiler_params=pltpu.CompilerParams(
            collective_id=0, has_side_effects=True, vmem_limit_bytes=40 * 2**20
        ),
    )(
        spin.reshape(3, 2 * NZ, LANES), region.reshape(2 * NZ, LANES), material.reshape(2 * NZ, LANES),
        saturation, anisotropy, damping, applied, demag_spectrum.reshape(6, 32, LY), *tables,
    )
    return rate.reshape(3, NZ, 2, LANES), demag.reshape(3, NZ, 2, LANES)


def solution(mesh):
    placed = (
        P(None, None, "wide", "narrow"),
        P(None, "wide", "narrow"),
        P(None, "wide", "narrow"),
        P(),
        P(),
        P(),
        P(),
        P(None, "wide", "narrow", None),
    )
    return jax.shard_map(
        shards,
        mesh=mesh,
        in_specs=placed,
        out_specs=(P(None, None, "wide", "narrow"), P(None, None, "wide", "narrow")),
        check_vma=False,
    )
```

```python
import functools
import math

import jax
import jax.numpy as jnp
import ml_dtypes
import numpy as np
from jax import lax
from jax.experimental import pallas as pl
from jax.experimental.pallas import tpu as pltpu
from jax.sharding import PartitionSpec as P

EXCHANGE = 0.3
MESH = pl.DeviceIdType.MESH
WIDE, NARROW = 64, 8
NZ, LZ, NX, LX, NY, LY = 32, 64, 128, 256, 1024, 2048
SLOTS = 32
ROWS = 32
K = 16
LANES = 128
F32, BF16 = jnp.float32, jnp.bfloat16
ROWS_OF = ((0, 3, 4), (3, 1, 5), (4, 5, 2))


def halves(x):
    hi = x.astype(np.float32).astype(ml_dtypes.bfloat16)
    lo = (x - hi.astype(np.float64)).astype(ml_dtypes.bfloat16)
    return np.stack([hi, lo])


def z_parts():
    s, z = np.arange(SLOTS)[:, None], np.arange(NZ)[None]
    angle = 2 * np.pi * (s * z % LZ) / LZ
    re = np.cos(angle)
    im = np.where(s == 0, np.where(z % 2, -1.0, 1.0), -np.sin(angle))
    return re, im


def z_forward():
    return np.concatenate(z_parts(), 0)


def z_inverse():
    re, im = z_parts()
    return np.concatenate([re, re, im, im], 0).T


def complex_matrix(angle):
    c, s = np.cos(angle), np.sin(angle)
    return np.block([[c, -s], [s, c]])


def x_angle():
    x = np.arange(NX).reshape(WIDE, 2).T.reshape(-1)
    return 2 * np.pi * (np.arange(NX)[:, None] * x[None] % LX) / LX


def y_angle():
    p = np.arange(LANES)
    return 2 * np.pi * (p[:, None] * p[None] % LANES) / LANES


def square_tables():
    angle = x_angle()
    tables = [
        complex_matrix(-angle),
        complex_matrix(angle.T) * (2.0 / (LZ * LX * LY)),
        complex_matrix(-y_angle()).T,
        complex_matrix(y_angle()).T,
    ]
    return np.stack([halves(t) for t in tables])


def y_twist():
    k, p = np.arange(K)[:, None], np.arange(LANES)[None]
    angle = 2 * np.pi * (k * p) / LY
    return np.stack([np.cos(angle), -np.sin(angle)]).astype(np.float32)


def mm(a, b):
    dot = functools.partial(jnp.dot, preferred_element_type=F32)
    return dot(a[0], b[0]) + (dot(a[0], b[1]) + dot(a[1], b[0]))


def split(x):
    hi = x.astype(BF16)
    return hi, (x - hi.astype(F32)).astype(BF16)


def turn(v, angle):
    c, s = math.cos(angle), math.sin(angle)
    re, im = v
    if abs(s) < 1e-9 and c > 0:
        return v
    if abs(c) < 1e-9:
        return (-im, re) if s > 0 else (im, -re)
    if abs(c - s) < 1e-9:
        return ((re - im) * c, (re + im) * c)
    if abs(c + s) < 1e-9:
        return ((re + im) * c, (im - re) * c)
    return (re * c - im * s, re * s + im * c)


def fft(values, direction):
    n = len(values)
    if n == 1:
        return values
    even = fft(values[0::2], direction)
    odd = fft(values[1::2], direction)
    odd = [turn(o, direction * 2 * math.pi * k / n) for k, o in enumerate(odd)]
    return ([(e[0] + o[0], e[1] + o[1]) for e, o in zip(even, odd)]
            + [(e[0] - o[0], e[1] - o[1]) for e, o in zip(even, odd)])


def shifted(x, step):
    zero = jnp.zeros((1, x.shape[1]), x.dtype)
    if step > 0:
        return jnp.concatenate([x[1:], zero], 0)
    return jnp.concatenate([zero, x[:-1]], 0)


def cross(x, y):
    return [x[1] * y[2] - x[2] * y[1], x[2] * y[0] - x[0] * y[2], x[0] * y[1] - x[1] * y[0]]


def pick(mat, table):
    out = jnp.full(mat.shape, table[3], F32)
    for i in range(3):
        out = jnp.where(mat == i, table[i], out)
    return out


def other_bit(bit, slot):
    return lax.rem(bit + slot, 2)


def kernel(spin_hbm, region_hbm, material_hbm, satur, aniso, damp, applied, spec_hbm,
           zf_hbm, zi_hbm, square_hbm, twist_hbm,
           rate_out, demag_out,
           spin, region, material, spec, zf, zi, square, twist,
           s1, r1, s2, r2, s3, r3, s4, r4, tensor, work, spectra, direction, satcell, base,
           hx_send, hx, hy_send, hy, spare_row, spare,
           load, send1, recv1, send2, recv2, send3, recv3, send4, recv4, hsend, hrecv):
    w, n = lax.axis_index("wide"), lax.axis_index("narrow")
    half, column = n // 4, lax.rem(n, 4)
    slot = lax.rem(w, SLOTS)
    part = other_bit(w // SLOTS, slot)
    special = slot == 0
    y_device = w <= SLOTS

    loads = [pltpu.make_async_copy(a, b, load.at[i]) for i, (a, b) in enumerate((
        (spin_hbm, spin), (region_hbm, region), (material_hbm, material), (zf_hbm, zf),
        (spec_hbm, spec), (square_hbm, square), (twist_hbm, twist), (zi_hbm, zi)))]
    for copy in loads:
        copy.start()

    def spectrum_device(i):
        return (lax.rem(i, SLOTS) + SLOTS * other_bit(half, i), 4 * (i // SLOTS) + column)

    def brick_device(i):
        return (i, 4 * part + column)

    def is_me(device):
        return (device[0] == w) & (device[1] == n)

    def line_device(i):
        return (jnp.where(i >= 4, SLOTS, slot), 4 * half + lax.rem(i, 4))

    def plane_device(i):
        return (slot + SLOTS * other_bit(i // 4, slot), 4 * half + lax.rem(i, 4))

    barrier = pltpu.get_barrier_semaphore()

    def greet(device):
        @pl.when(jnp.logical_not(is_me(device)))
        def _():
            pl.semaphore_signal(barrier, inc=1, device_id=device, device_id_type=MESH)

    def greet_all(count, device):
        def go(i, carry):
            greet(device(i))
            return carry
        lax.fori_loop(0, count, go, 0)

    greet_all(64, spectrum_device)
    greet_all(64, brick_device)
    greet_all(jnp.where(special, 8, 4), line_device)

    @pl.when(y_device)
    def _():
        greet_all(8, plane_device)

    sides = [(lax.rem(w + 1, WIDE), n), (lax.rem(w + WIDE - 1, WIDE), n),
             (w, lax.rem(n + 1, NARROW)), (w, lax.rem(n + NARROW - 1, NARROW))]
    for device in sides:
        greet(device)
    on_both = half == part
    expected = (128 - 2 * jnp.where(on_both, 1, 0)
                + jnp.where(special, 8, 4) - jnp.where(w <= SLOTS, 1, 0)
                + jnp.where(y_device, 7, 0) + 4)

    for copy in loads[:4]:
        copy.wait()
    for xx in range(2):
        rows = pl.ds(xx, NZ, stride=2)
        mag = region[rows, :].astype(F32)
        satcell[xx] = pick(material[rows, :], satur)
        for c in range(3):
            direction[c, xx] = spin[c, rows, :] * mag
    for c in range(3):
        moment = jnp.concatenate([direction[c, xx] * satcell[xx] for xx in range(2)], 1)
        out = mm((zf[0], zf[1]), split(moment))
        s1[:, 512 * c:512 * c + 256] = out[:SLOTS]
        s1[:, 512 * c + 256:512 * c + 512] = out[SLOTS:]

    lane = lax.broadcasted_iota(jnp.int32, (NZ, LANES), 1)
    for xx in range(2):
        for c in range(3):
            hx_send[1 - xx, NZ * c:NZ * c + NZ, :] = direction[c, xx]
        for side, at in ((0, LANES - 1), (1, 0)):
            cols = [jnp.broadcast_to(direction[c, xx][:, at:at + 1], (NZ, LANES)) for c in range(3)]
            hy_send[side, NZ * xx:NZ * xx + NZ, :] = jnp.where(
                lane == 0, cols[0], jnp.where(lane == 1, cols[1], cols[2]))

    pl.semaphore_wait(barrier, expected)

    def local(src, dst, sem):
        return pltpu.make_async_copy(src, dst, sem)

    def put(src, dst, dump, send, recv, device):
        @pl.when(is_me(device))
        def _():
            local(src, dst, recv).start()
            local(src, dump, send).start()

        @pl.when(jnp.logical_not(is_me(device)))
        def _():
            pltpu.make_async_remote_copy(
                src, dst, send, recv, device_id=device, device_id_type=MESH).start()

    def done(ref, sem):
        local(ref, ref, sem).wait()


    def spectra_start():
        def go(step, carry):
            i = lax.rem(w + step, 64)
            put(s1.at[pl.ds(lax.rem(i, SLOTS), 1)], r1.at[pl.ds(w, 1)], spare_row.at[pl.ds(0, 1)],
                send1, recv1, spectrum_device(i))
            return carry
        lax.fori_loop(0, 64, go, 0)

    def bricks_start():
        def go(step, carry):
            i = lax.rem(w + step, 64)
            put(s4.at[pl.ds(i, 1)], r4.at[pl.ds(SLOTS * half + slot, 1)], spare_row.at[pl.ds(8, 1)],
                send4, recv4, brick_device(i))
            return carry
        lax.fori_loop(0, 64, go, 0)

    def lines_start(c):
        def go(i, carry):
            put(s2.at[c, i], r2.at[c, 4 * part + column], spare.at[c], send2.at[c], recv2.at[c], line_device(i))
            return carry
        lax.fori_loop(0, jnp.where(special, 8, 4), go, 0)

    def planes_start(c):
        def go(i, carry):
            put(s3.at[c, i], r3.at[c, column + jnp.where(w == SLOTS, 4, 0)], spare.at[3 + c],
                send3.at[c], recv3.at[c], plane_device(i))
            return carry
        lax.fori_loop(0, 8, go, 0)

    def done_blocks(ref, sem):
        @pl.when(special)
        def _():
            done(ref, sem)

        @pl.when(jnp.logical_not(special))
        def _():
            done(ref.at[pl.ds(0, 4)], sem)

    halo = [pltpu.make_async_remote_copy(
        src, dst, hsend.at[i], hrecv.at[i], device_id=sides[i], device_id_type=MESH)
        for i, (src, dst) in enumerate((
            (hx_send.at[0], hx.at[0]), (hx_send.at[1], hx.at[1]),
            (hy_send.at[0], hy.at[0]), (hy_send.at[1], hy.at[1])))]

    spectra_start()
    for copy in halo:
        copy.start()
    for copy in loads[4:]:
        copy.wait()

    @pl.when(y_device)
    def _():
        flat = spec[...].reshape(6 * ROWS, LY)

        def reorder(k, carry):
            ky = lax.broadcasted_iota(jnp.int32, (LY, LANES), 0)
            col = lax.broadcasted_iota(jnp.int32, (LY, LANES), 1)
            choose = jnp.where(ky == K * col + k, 1.0, 0.0).astype(BF16)
            got = jnp.dot(flat, choose, preferred_element_type=F32)
            for g in range(6):
                for t in range(4):
                    tensor[g, pl.ds(pl.multiple_of(128 * t + 8 * k, 8), 8), :] = (
                        got[ROWS * g + 8 * t:ROWS * g + 8 * t + 8])
            return carry

        lax.fori_loop(0, K, reorder, 0)

    flip = jnp.where(half == 1, -1.0, 1.0).astype(F32)

    def x_forward(c):
        got = r1[:, 512 * c:512 * c + 512]
        re = jnp.concatenate([got[:, 0:128], got[:, 128:256] * flip], 0)
        im = jnp.concatenate([got[:, 256:384], got[:, 384:512] * flip], 0)
        rhs = jnp.concatenate([re, jnp.where(special, jnp.zeros_like(im), im)], 0)

        def store(out, at):
            for i in range(4):
                s2[c, at + i, :, 0:128] = out[ROWS * i:ROWS * i + ROWS]
                s2[c, at + i, :, 128:256] = out[128 + ROWS * i:128 + ROWS * i + ROWS]

        store(mm((square[0, 0], square[0, 1]), split(rhs)), 0)

        @pl.when(special)
        def _():
            other = jnp.concatenate([im, jnp.zeros_like(im)], 0)
            store(mm((square[0, 0], square[0, 1]), split(other)), 4)

        lines_start(c)

    done(r1, recv1)
    for c in range(3):
        x_forward(c)

    def y_forward(c):
        done(r2.at[c], recv2.at[c])

        def go(t, carry):
            rows = pl.ds(pl.multiple_of(8 * t, 8), 8)
            v = [(r2[c, b, rows, 0:128], r2[c, b, rows, 128:256]) for b in range(8)]
            even = fft(v, -1)
            odd = fft([turn(x, -2 * math.pi * b / K) for b, x in enumerate(v)], -1)
            for k in range(K):
                re, im = even[k // 2] if k % 2 == 0 else odd[k // 2]
                cos, sin = twist[0, k:k + 1, :], twist[1, k:k + 1, :]
                at = pl.ds(pl.multiple_of(128 * t + 8 * k, 8), 8)
                work[at, 0:128] = re * cos - im * sin
                work[at, 128:256] = re * sin + im * cos
            return carry

        lax.fori_loop(0, 4, go, 0)

        def multiply(t, carry):
            rows = pl.ds(pl.multiple_of(256 * t, 256), 256)
            spectra[c, rows, :] = mm(split(work[rows, :]), (square[2, 0], square[2, 1]))
            return carry

        lax.fori_loop(0, 2, multiply, 0)

    def y_inverse(c):
        a, b, d = ROWS_OF[c]

        def multiply(t, carry):
            rows = pl.ds(pl.multiple_of(256 * t, 256), 256)
            field = [-(tensor[a, rows, :] * spectra[0, rows, at:at + 128]
                       + tensor[b, rows, :] * spectra[1, rows, at:at + 128]
                       + tensor[d, rows, :] * spectra[2, rows, at:at + 128]) for at in (0, 128)]
            work[rows, :] = mm(split(jnp.concatenate(field, 1)), (square[3, 0], square[3, 1]))
            return carry

        lax.fori_loop(0, 2, multiply, 0)

        def go(t, carry):
            u = []
            for k in range(K):
                at = pl.ds(pl.multiple_of(128 * t + 8 * k, 8), 8)
                re, im = work[at, 0:128], work[at, 128:256]
                cos, sin = twist[0, k:k + 1, :], twist[1, k:k + 1, :]
                u.append((re * cos + im * sin, im * cos - re * sin))
            even = fft(u[0::2], 1)
            odd = fft(u[1::2], 1)
            rows = pl.ds(pl.multiple_of(8 * t, 8), 8)
            for j in range(8):
                o = turn(odd[j], 2 * math.pi * j / K)
                s3[c, j, rows, 0:128] = even[j][0] + o[0]
                s3[c, j, rows, 128:256] = even[j][1] + o[1]
            return carry

        lax.fori_loop(0, 4, go, 0)
        planes_start(c)

    def x_inverse(c):
        done_blocks(r3.at[c], recv3.at[c])

        def transform(at):
            got = r3[c, at:at + 4].reshape(4 * ROWS, 256)
            rhs = jnp.concatenate([got[:, 0:128], got[:, 128:256]], 0)
            return mm((square[1, 0], square[1, 1]), split(rhs))

        def store(out, at):
            at += 512 * c
            s4[:, at:at + 128] = out[:WIDE]
            s4[:, at + 128:at + 256] = out[WIDE:] * flip

        out = transform(0) * jnp.where(special, 0.5, 1.0).astype(F32)
        store(out[:NX], 0)

        @pl.when(jnp.logical_not(special))
        def _():
            store(out[NX:], 256)

        @pl.when(special)
        def _():
            store(transform(4)[:NX] * 0.5, 256)

    @pl.when(y_device)
    def _():
        for c in range(3):
            y_forward(c)
        y_inverse(0)
        y_inverse(1)

    x_inverse(0)

    @pl.when(y_device)
    def _():
        y_inverse(2)

    x_inverse(1)
    x_inverse(2)
    bricks_start()

    for copy in halo:
        copy.wait()
    inside = [jnp.where(w > 0, 1.0, 0.0), jnp.where(w < WIDE - 1, 1.0, 0.0),
              jnp.where(n > 0, 1.0, 0.0), jnp.where(n < NARROW - 1, 1.0, 0.0)]
    for xx in range(2):
        total = [jnp.zeros((NZ, LANES), F32)] * 3
        weight = jnp.zeros((NZ, LANES), F32)
        here = [direction[c, xx] for c in range(3)]
        sat = satcell[xx]

        def x_halo(side):
            return [hx[side, NZ * c:NZ * c + NZ, :] * inside[side] for c in range(3)]

        def y_edge(side, c):
            edge = hy[side, NZ * xx:NZ * xx + NZ, c:c + 1] * inside[2 + side]
            return jnp.broadcast_to(edge, (NZ, LANES))

        neighbours = [
            [shifted(d, 1) for d in here],
            [shifted(d, -1) for d in here],
            [direction[c, 0] for c in range(3)] if xx == 1 else x_halo(0),
            [direction[c, 1] for c in range(3)] if xx == 0 else x_halo(1),
            [jnp.where(lane == LANES - 1, y_edge(1, c), pltpu.roll(here[c], LANES - 1, 1)) for c in range(3)],
            [jnp.where(lane == 0, y_edge(0, c), pltpu.roll(here[c], 1, 1)) for c in range(3)],
        ]
        for near in neighbours:
            total = [a + b for a, b in zip(total, near)]
            weight = weight + (near[0] * near[0] + near[1] * near[1] + near[2] * near[2])
        anis = pick(material[pl.ds(xx, NZ, stride=2), :], aniso)
        for c in range(3):
            field = EXCHANGE * (total[c] - weight * here[c]) / sat + applied[c]
            if c == 2:
                field = field + 2.0 * anis / sat * here[2]
            base[c, xx] = field

    done(r4, recv4)
    for c in range(3):
        got = r4[:, 512 * c:512 * c + 512]
        rhs = jnp.concatenate([got[:, 0:256], got[:, 256:512]], 0)
        out = mm((zi[0], zi[1]), split(rhs))
        for xx in range(2):
            h = out[:, LANES * xx:LANES * xx + LANES]
            demag_out[c, pl.ds(xx, NZ, stride=2), :] = h
            base[c, xx] = base[c, xx] + h
    for xx in range(2):
        rows = pl.ds(xx, NZ, stride=2)
        a = pick(material[rows, :], damp)
        d = [direction[c, xx] for c in range(3)]
        torque = cross(d, [base[c, xx] for c in range(3)])
        second = cross(d, torque)
        for c in range(3):
            rate_out[c, rows, :] = -(torque[c] + a * second[c]) / (1.0 + a * a)

    done(r1, send1)
    done(s4, send4)
    for c in range(3):
        done_blocks(s2.at[c], send2.at[c])

    @pl.when(y_device)
    def _():
        for c in range(3):
            done(s3.at[c], send3.at[c])


def shards(spin, region, material, saturation, anisotropy, damping, applied, demag_spectrum):
    vmem = pl.BlockSpec(memory_space=pltpu.VMEM)
    smem = pl.BlockSpec(memory_space=pltpu.SMEM)
    hbm = pl.BlockSpec(memory_space=pltpu.HBM)
    tables = [jnp.asarray(t) for t in (halves(z_forward()), halves(z_inverse()), square_tables(), y_twist())]
    dma = pltpu.SemaphoreType.DMA
    out = jax.ShapeDtypeStruct((3, 2 * NZ, LANES), F32)
    big = [spin.reshape(3, 2 * NZ, LANES), region.reshape(2 * NZ, LANES), material.reshape(2 * NZ, LANES)]
    spec = demag_spectrum.reshape(6, ROWS, LY)

    def room(x):
        return pltpu.VMEM(x.shape, x.dtype)

    rate, demag = pl.pallas_call(
        kernel,
        out_shape=(out, out),
        in_specs=[hbm] * 3 + [smem] * 4 + [hbm] * (1 + len(tables)),
        out_specs=(vmem, vmem),
        scratch_shapes=[room(x) for x in big + [spec] + tables]
        + [
            pltpu.VMEM((SLOTS, 1536), F32),
            pltpu.VMEM((64, 1536), F32),
        ]
        + [pltpu.VMEM((3, 8, ROWS, 256), F32)] * 4
        + [pltpu.VMEM((64, 1536), F32)] * 2
        + [
            pltpu.VMEM((6, 512, LANES), F32),
            pltpu.VMEM((512, 256), F32),
            pltpu.VMEM((3, 512, 256), F32),
            pltpu.VMEM((3, 2, NZ, LANES), F32),
            pltpu.VMEM((2, NZ, LANES), F32),
            pltpu.VMEM((3, 2, NZ, LANES), F32),
            pltpu.VMEM((2, 3 * NZ, LANES), F32),
            pltpu.VMEM((2, 3 * NZ, LANES), F32),
            pltpu.VMEM((2, 2 * NZ, LANES), F32),
            pltpu.VMEM((2, 2 * NZ, LANES), F32),
            pltpu.VMEM((16, 1536), F32),
            pltpu.VMEM((6, ROWS, 256), F32),
        ]
        + [dma((8,))]
        + [dma] * 2 + [dma((3,))] * 4 + [dma] * 2
        + [dma((4,)), dma((4,))],
        compiler_params=pltpu.CompilerParams(
            collective_id=0, has_side_effects=True, vmem_limit_bytes=56 * 2**20
        ),
    )(*big, saturation, anisotropy, damping, applied, spec, *tables)
    return rate.reshape(3, NZ, 2, LANES), demag.reshape(3, NZ, 2, LANES)


def solution(mesh):
    placed = (
        P(None, None, "wide", "narrow"),
        P(None, "wide", "narrow"),
        P(None, "wide", "narrow"),
        P(),
        P(),
        P(),
        P(),
        P(None, "wide", "narrow", None),
    )
    return jax.shard_map(
        shards,
        mesh=mesh,
        in_specs=placed,
        out_specs=(P(None, None, "wide", "narrow"), P(None, None, "wide", "narrow")),
        check_vma=False,
    )
```

```python
import functools
import math

import jax
import jax.numpy as jnp
import ml_dtypes
import numpy as np
from jax import lax
from jax.experimental import pallas as pl
from jax.experimental.pallas import tpu as pltpu
from jax.sharding import PartitionSpec as P

EXCHANGE = 0.3
MESH = pl.DeviceIdType.MESH
WIDE, NARROW = 64, 8
NZ, LZ, NX, LX, NY, LY = 32, 64, 128, 256, 1024, 2048
SLOTS = 32
ROWS = 32
K = 16
LANES = 128
UNROLL = 9
S1_CHUNKS = ((0, 1), (2,))
S4_CHUNKS = ((0,), (1, 2))
F32, BF16 = jnp.float32, jnp.bfloat16
ROWS_OF = ((0, 3, 4), (3, 1, 5), (4, 5, 2))


def halves(x):
    hi = x.astype(np.float32).astype(ml_dtypes.bfloat16)
    lo = (x - hi.astype(np.float64)).astype(ml_dtypes.bfloat16)
    return np.stack([hi, lo])


def z_parts():
    s, z = np.arange(SLOTS)[:, None], np.arange(NZ)[None]
    angle = 2 * np.pi * (s * z % LZ) / LZ
    re = np.cos(angle)
    im = np.where(s == 0, np.where(z % 2, -1.0, 1.0), -np.sin(angle))
    return re, im


def z_forward():
    return np.concatenate(z_parts(), 0)


def z_inverse():
    re, im = z_parts()
    return np.concatenate([re, re, im, im], 0).T


def complex_matrix(angle):
    c, s = np.cos(angle), np.sin(angle)
    return np.block([[c, -s], [s, c]])


def x_angle():
    x = np.arange(NX).reshape(WIDE, 2).T.reshape(-1)
    return 2 * np.pi * (np.arange(NX)[:, None] * x[None] % LX) / LX


def y_angle():
    p = np.arange(LANES)
    return 2 * np.pi * (p[:, None] * p[None] % LANES) / LANES


def square_tables():
    angle = x_angle()
    tables = [
        complex_matrix(-angle),
        complex_matrix(angle.T) * (2.0 / (LZ * LX * LY)),
        complex_matrix(-y_angle()).T,
        complex_matrix(y_angle()).T,
    ]
    return np.stack([halves(t) for t in tables])


def y_twist():
    k, p = np.arange(K)[:, None], np.arange(LANES)[None]
    angle = 2 * np.pi * (k * p) / LY
    return np.stack([np.cos(angle), -np.sin(angle)]).astype(np.float32)


def mm(a, b):
    dot = functools.partial(jnp.dot, preferred_element_type=F32)
    return dot(a[0], b[0]) + (dot(a[0], b[1]) + dot(a[1], b[0]))


def split(x):
    hi = x.astype(BF16)
    return hi, (x - hi.astype(F32)).astype(BF16)


def turn(v, angle):
    c, s = math.cos(angle), math.sin(angle)
    re, im = v
    if abs(s) < 1e-9 and c > 0:
        return v
    if abs(c) < 1e-9:
        return (-im, re) if s > 0 else (im, -re)
    if abs(c - s) < 1e-9:
        return ((re - im) * c, (re + im) * c)
    if abs(c + s) < 1e-9:
        return ((re + im) * c, (im - re) * c)
    return (re * c - im * s, re * s + im * c)


def fft(values, direction):
    n = len(values)
    if n == 1:
        return values
    even = fft(values[0::2], direction)
    odd = fft(values[1::2], direction)
    odd = [turn(o, direction * 2 * math.pi * k / n) for k, o in enumerate(odd)]
    return ([(e[0] + o[0], e[1] + o[1]) for e, o in zip(even, odd)]
            + [(e[0] - o[0], e[1] - o[1]) for e, o in zip(even, odd)])


def shifted(x, step):
    zero = jnp.zeros((1, x.shape[1]), x.dtype)
    if step > 0:
        return jnp.concatenate([x[1:], zero], 0)
    return jnp.concatenate([zero, x[:-1]], 0)


def cross(x, y):
    return [x[1] * y[2] - x[2] * y[1], x[2] * y[0] - x[0] * y[2], x[0] * y[1] - x[1] * y[0]]


def pick(mat, table):
    out = jnp.full(mat.shape, table[3], F32)
    for i in range(3):
        out = jnp.where(mat == i, table[i], out)
    return out


def other_bit(bit, slot):
    return lax.rem(bit + slot, 2)


def kernel(spin_hbm, region_hbm, material_hbm, satur, aniso, damp, applied, spec_hbm,
           zf_hbm, zi_hbm, square_hbm, twist_hbm,
           rate_out, demag_out,
           spin, region, material, spec, zf, zi, square, twist,
           s1, r1, s2, r2, s3, r3, s4, r4, tensor, work, spectra, direction, satcell, base,
           hx_send, hx, hy_send, hy, spare_row, spare,
           load, send1, recv1, send2, recv2, send3, recv3, send4, recv4, hsend, hrecv):
    w, n = lax.axis_index("wide"), lax.axis_index("narrow")
    half, column = n // 4, lax.rem(n, 4)
    slot = lax.rem(w, SLOTS)
    part = other_bit(w // SLOTS, slot)
    special = slot == 0
    y_device = w <= SLOTS

    loads = [pltpu.make_async_copy(a, b, load.at[i]) for i, (a, b) in enumerate((
        (spin_hbm, spin), (region_hbm, region), (material_hbm, material), (zf_hbm, zf),
        (spec_hbm, spec), (square_hbm, square), (twist_hbm, twist), (zi_hbm, zi)))]
    for copy in loads:
        copy.start()

    def spectrum_device(i):
        return (lax.rem(i, SLOTS) + SLOTS * other_bit(half, i), 4 * (i // SLOTS) + column)

    def brick_device(i):
        return (i, 4 * part + column)

    def is_me(device):
        return (device[0] == w) & (device[1] == n)

    def line_device(i):
        return (jnp.where(i >= 4, SLOTS, slot), 4 * half + lax.rem(i, 4))

    def plane_device(i):
        return (slot + SLOTS * other_bit(i // 4, slot), 4 * half + lax.rem(i, 4))

    barrier = pltpu.get_barrier_semaphore()

    def signal(device):
        pl.semaphore_signal(barrier, inc=1, device_id=device, device_id_type=MESH)

    def greet(device):
        @pl.when(jnp.logical_not(is_me(device)))
        def _():
            signal(device)

    def greet_all(count, device):
        def go(i, carry):
            greet(device(i))
            return carry
        lax.fori_loop(0, count, go, 0)

    on_both = half == part

    def greet_brick(i, carry):
        signal(brick_device(lax.rem(w + i, WIDE)))
        return carry

    @pl.when(jnp.logical_not(on_both))
    def _():
        signal(brick_device(w))
    lax.fori_loop(1, WIDE, greet_brick, 0, unroll=UNROLL)

    def greet_spectrum(i, carry):
        signal(spectrum_device(SLOTS * (1 - part) + i))
        return carry
    lax.fori_loop(0, SLOTS, greet_spectrum, 0, unroll=8)
    greet_all(jnp.where(special, 8, 4), line_device)

    @pl.when(y_device)
    def _():
        greet_all(8, plane_device)

    sides = [(lax.rem(w + 1, WIDE), n), (lax.rem(w + WIDE - 1, WIDE), n),
             (w, lax.rem(n + 1, NARROW)), (w, lax.rem(n + NARROW - 1, NARROW))]
    for device in sides:
        greet(device)
    expected = (96 - jnp.where(on_both, 1, 0)
                + jnp.where(special, 8, 4) - jnp.where(w <= SLOTS, 1, 0)
                + jnp.where(y_device, 7, 0) + 4)

    for copy in loads[:4]:
        copy.wait()
    for xx in range(2):
        rows = pl.ds(xx, NZ, stride=2)
        mag = region[rows, :].astype(F32)
        satcell[xx] = pick(material[rows, :], satur)
        for c in range(3):
            direction[c, xx] = spin[c, rows, :] * mag
    for c in range(3):
        moment = jnp.concatenate([direction[c, xx] * satcell[xx] for xx in range(2)], 1)
        out = mm((zf[0], zf[1]), split(moment))
        s1[:, 512 * c:512 * c + 256] = out[:SLOTS]
        s1[:, 512 * c + 256:512 * c + 512] = out[SLOTS:]

    lane = lax.broadcasted_iota(jnp.int32, (NZ, LANES), 1)
    for xx in range(2):
        for c in range(3):
            hx_send[1 - xx, NZ * c:NZ * c + NZ, :] = direction[c, xx]
        for side, at in ((0, LANES - 1), (1, 0)):
            cols = [jnp.broadcast_to(direction[c, xx][:, at:at + 1], (NZ, LANES)) for c in range(3)]
            hy_send[side, NZ * xx:NZ * xx + NZ, :] = jnp.where(
                lane == 0, cols[0], jnp.where(lane == 1, cols[1], cols[2]))

    pl.semaphore_wait(barrier, expected)

    def local(src, dst, sem):
        return pltpu.make_async_copy(src, dst, sem)

    def put(src, dst, dump, send, recv, device):
        @pl.when(is_me(device))
        def _():
            local(src, dst, recv).start()
            local(src, dump, send).start()

        @pl.when(jnp.logical_not(is_me(device)))
        def _():
            pltpu.make_async_remote_copy(
                src, dst, send, recv, device_id=device, device_id_type=MESH).start()

    def done(ref, sem):
        local(ref, ref, sem).wait()


    def columns(chunk):
        return pl.ds(512 * chunk[0], 512 * len(chunk))

    def scatter(count, first, src_row, src, dst, dst_row, dump, cols, send, recv, device):
        def copy(i):
            return pltpu.make_async_remote_copy(
                src.at[pl.ds(src_row(i), 1), cols], dst.at[pl.ds(dst_row, 1), cols], send, recv,
                device_id=device(i), device_id_type=MESH)

        def go(step, carry):
            copy(lax.rem(first + step, count)).start()
            return carry

        lax.fori_loop(1, count, go, 0, unroll=UNROLL)

        @pl.when(on_both)
        def _():
            own = src.at[pl.ds(src_row(first), 1), cols]
            local(own, dst.at[pl.ds(dst_row, 1), cols], recv).start()
            local(own, spare_row.at[pl.ds(dump, 1), cols], send).start()

        @pl.when(jnp.logical_not(on_both))
        def _():
            copy(first).start()

    def spectra_start(g, chunk):
        scatter(64, SLOTS * half + slot, lambda i: lax.rem(i, SLOTS), s1, r1, w, 0, columns(chunk),
                send1.at[g], recv1.at[g], spectrum_device)

    def bricks_start(g, chunk):
        scatter(64, w, lambda i: i, s4, r4, SLOTS * half + slot, 8, columns(chunk),
                send4.at[g], recv4.at[g], brick_device)

    def lines_start(c):
        def go(i, carry):
            put(s2.at[c, i], r2.at[c, 4 * part + column], spare.at[c], send2.at[c], recv2.at[c], line_device(i))
            return carry
        lax.fori_loop(0, jnp.where(special, 8, 4), go, 0)

    def planes_start(c):
        def go(i, carry):
            put(s3.at[c, i], r3.at[c, column + jnp.where(w == SLOTS, 4, 0)], spare.at[3 + c],
                send3.at[c], recv3.at[c], plane_device(i))
            return carry
        lax.fori_loop(0, 8, go, 0)

    def done_blocks(ref, sem):
        @pl.when(special)
        def _():
            done(ref, sem)

        @pl.when(jnp.logical_not(special))
        def _():
            done(ref.at[pl.ds(0, 4)], sem)

    halo = [pltpu.make_async_remote_copy(
        src, dst, hsend.at[i], hrecv.at[i], device_id=sides[i], device_id_type=MESH)
        for i, (src, dst) in enumerate((
            (hx_send.at[0], hx.at[0]), (hx_send.at[1], hx.at[1]),
            (hy_send.at[0], hy.at[0]), (hy_send.at[1], hy.at[1])))]

    for g, chunk in enumerate(S1_CHUNKS):
        spectra_start(g, chunk)
    for copy in halo:
        copy.start()
    for copy in loads[4:]:
        copy.wait()

    @pl.when(y_device)
    def _():
        flat = spec[...].reshape(6 * ROWS, LY)

        def reorder(k, carry):
            ky = lax.broadcasted_iota(jnp.int32, (LY, LANES), 0)
            col = lax.broadcasted_iota(jnp.int32, (LY, LANES), 1)
            choose = jnp.where(ky == K * col + k, 1.0, 0.0).astype(BF16)
            got = jnp.dot(flat, choose, preferred_element_type=F32)
            for g in range(6):
                for t in range(4):
                    tensor[g, pl.ds(pl.multiple_of(128 * t + 8 * k, 8), 8), :] = (
                        got[ROWS * g + 8 * t:ROWS * g + 8 * t + 8])
            return carry

        lax.fori_loop(0, K, reorder, 0)

    flip = jnp.where(half == 1, -1.0, 1.0).astype(F32)

    def x_forward(c):
        got = r1[:, 512 * c:512 * c + 512]
        re = jnp.concatenate([got[:, 0:128], got[:, 128:256] * flip], 0)
        im = jnp.concatenate([got[:, 256:384], got[:, 384:512] * flip], 0)
        rhs = jnp.concatenate([re, jnp.where(special, jnp.zeros_like(im), im)], 0)

        def store(out, at):
            for i in range(4):
                s2[c, at + i, :, 0:128] = out[ROWS * i:ROWS * i + ROWS]
                s2[c, at + i, :, 128:256] = out[128 + ROWS * i:128 + ROWS * i + ROWS]

        store(mm((square[0, 0], square[0, 1]), split(rhs)), 0)

        @pl.when(special)
        def _():
            other = jnp.concatenate([im, jnp.zeros_like(im)], 0)
            store(mm((square[0, 0], square[0, 1]), split(other)), 4)

        lines_start(c)

    def y_forward(c):
        done(r2.at[c], recv2.at[c])

        def go(t, carry):
            rows = pl.ds(pl.multiple_of(8 * t, 8), 8)
            v = [(r2[c, b, rows, 0:128], r2[c, b, rows, 128:256]) for b in range(8)]
            even = fft(v, -1)
            odd = fft([turn(x, -2 * math.pi * b / K) for b, x in enumerate(v)], -1)
            for k in range(K):
                re, im = even[k // 2] if k % 2 == 0 else odd[k // 2]
                cos, sin = twist[0, k:k + 1, :], twist[1, k:k + 1, :]
                at = pl.ds(pl.multiple_of(128 * t + 8 * k, 8), 8)
                work[at, 0:128] = re * cos - im * sin
                work[at, 128:256] = re * sin + im * cos
            return carry

        lax.fori_loop(0, 4, go, 0)

        def multiply(t, carry):
            rows = pl.ds(pl.multiple_of(256 * t, 256), 256)
            spectra[c, rows, :] = mm(split(work[rows, :]), (square[2, 0], square[2, 1]))
            return carry

        lax.fori_loop(0, 2, multiply, 0)

    def ahead(chunk):
        @pl.when(y_device)
        def _():
            for c in chunk:
                y_forward(c)

    for g, chunk in enumerate(S1_CHUNKS):
        done(r1.at[:, columns(chunk)], recv1.at[g])
        for c in chunk:
            x_forward(c)
        if g:
            ahead(S1_CHUNKS[g - 1])
    ahead(S1_CHUNKS[-1])

    def y_inverse(c):
        a, b, d = ROWS_OF[c]

        def multiply(t, carry):
            rows = pl.ds(pl.multiple_of(256 * t, 256), 256)
            field = [-(tensor[a, rows, :] * spectra[0, rows, at:at + 128]
                       + tensor[b, rows, :] * spectra[1, rows, at:at + 128]
                       + tensor[d, rows, :] * spectra[2, rows, at:at + 128]) for at in (0, 128)]
            work[rows, :] = mm(split(jnp.concatenate(field, 1)), (square[3, 0], square[3, 1]))
            return carry

        lax.fori_loop(0, 2, multiply, 0)

        def go(t, carry):
            u = []
            for k in range(K):
                at = pl.ds(pl.multiple_of(128 * t + 8 * k, 8), 8)
                re, im = work[at, 0:128], work[at, 128:256]
                cos, sin = twist[0, k:k + 1, :], twist[1, k:k + 1, :]
                u.append((re * cos + im * sin, im * cos - re * sin))
            even = fft(u[0::2], 1)
            odd = fft(u[1::2], 1)
            rows = pl.ds(pl.multiple_of(8 * t, 8), 8)
            for j in range(8):
                o = turn(odd[j], 2 * math.pi * j / K)
                s3[c, j, rows, 0:128] = even[j][0] + o[0]
                s3[c, j, rows, 128:256] = even[j][1] + o[1]
            return carry

        lax.fori_loop(0, 4, go, 0)
        planes_start(c)

    def x_inverse(c):
        done_blocks(r3.at[c], recv3.at[c])

        def transform(at):
            got = r3[c, at:at + 4].reshape(4 * ROWS, 256)
            rhs = jnp.concatenate([got[:, 0:128], got[:, 128:256]], 0)
            return mm((square[1, 0], square[1, 1]), split(rhs))

        def store(out, at):
            at += 512 * c
            s4[:, at:at + 128] = out[:WIDE]
            s4[:, at + 128:at + 256] = out[WIDE:] * flip

        out = transform(0) * jnp.where(special, 0.5, 1.0).astype(F32)
        store(out[:NX], 0)

        @pl.when(jnp.logical_not(special))
        def _():
            store(out[NX:], 256)

        @pl.when(special)
        def _():
            store(transform(4)[:NX] * 0.5, 256)

        for g, chunk in enumerate(S4_CHUNKS):
            if c == chunk[-1]:
                bricks_start(g, chunk)

    @pl.when(y_device)
    def _():
        y_inverse(0)
        y_inverse(1)

    x_inverse(0)

    @pl.when(y_device)
    def _():
        y_inverse(2)

    x_inverse(1)
    x_inverse(2)

    for copy in halo:
        copy.wait()
    inside = [jnp.where(w > 0, 1.0, 0.0), jnp.where(w < WIDE - 1, 1.0, 0.0),
              jnp.where(n > 0, 1.0, 0.0), jnp.where(n < NARROW - 1, 1.0, 0.0)]
    for xx in range(2):
        total = [jnp.zeros((NZ, LANES), F32)] * 3
        weight = jnp.zeros((NZ, LANES), F32)
        here = [direction[c, xx] for c in range(3)]
        sat = satcell[xx]

        def x_halo(side):
            return [hx[side, NZ * c:NZ * c + NZ, :] * inside[side] for c in range(3)]

        def y_edge(side, c):
            edge = hy[side, NZ * xx:NZ * xx + NZ, c:c + 1] * inside[2 + side]
            return jnp.broadcast_to(edge, (NZ, LANES))

        neighbours = [
            [shifted(d, 1) for d in here],
            [shifted(d, -1) for d in here],
            [direction[c, 0] for c in range(3)] if xx == 1 else x_halo(0),
            [direction[c, 1] for c in range(3)] if xx == 0 else x_halo(1),
            [jnp.where(lane == LANES - 1, y_edge(1, c), pltpu.roll(here[c], LANES - 1, 1)) for c in range(3)],
            [jnp.where(lane == 0, y_edge(0, c), pltpu.roll(here[c], 1, 1)) for c in range(3)],
        ]
        for near in neighbours:
            total = [a + b for a, b in zip(total, near)]
            weight = weight + (near[0] * near[0] + near[1] * near[1] + near[2] * near[2])
        anis = pick(material[pl.ds(xx, NZ, stride=2), :], aniso)
        for c in range(3):
            field = EXCHANGE * (total[c] - weight * here[c]) / sat + applied[c]
            if c == 2:
                field = field + 2.0 * anis / sat * here[2]
            base[c, xx] = field

    for c in range(3):
        for g, chunk in enumerate(S4_CHUNKS):
            if c == chunk[0]:
                done(r4.at[:, columns(chunk)], recv4.at[g])
        got = r4[:, 512 * c:512 * c + 512]
        rhs = jnp.concatenate([got[:, 0:256], got[:, 256:512]], 0)
        out = mm((zi[0], zi[1]), split(rhs))
        for xx in range(2):
            h = out[:, LANES * xx:LANES * xx + LANES]
            demag_out[c, pl.ds(xx, NZ, stride=2), :] = h
            base[c, xx] = base[c, xx] + h
    for xx in range(2):
        rows = pl.ds(xx, NZ, stride=2)
        a = pick(material[rows, :], damp)
        d = [direction[c, xx] for c in range(3)]
        torque = cross(d, [base[c, xx] for c in range(3)])
        second = cross(d, torque)
        for c in range(3):
            rate_out[c, rows, :] = -(torque[c] + a * second[c]) / (1.0 + a * a)

    for g, chunk in enumerate(S1_CHUNKS):
        done(r1.at[:, columns(chunk)], send1.at[g])
    for g, chunk in enumerate(S4_CHUNKS):
        done(s4.at[:, columns(chunk)], send4.at[g])
    for c in range(3):
        done_blocks(s2.at[c], send2.at[c])

    @pl.when(y_device)
    def _():
        for c in range(3):
            done(s3.at[c], send3.at[c])


def shards(spin, region, material, saturation, anisotropy, damping, applied, demag_spectrum):
    vmem = pl.BlockSpec(memory_space=pltpu.VMEM)
    smem = pl.BlockSpec(memory_space=pltpu.SMEM)
    hbm = pl.BlockSpec(memory_space=pltpu.HBM)
    tables = [jnp.asarray(t) for t in (halves(z_forward()), halves(z_inverse()), square_tables(), y_twist())]
    dma = pltpu.SemaphoreType.DMA
    out = jax.ShapeDtypeStruct((3, 2 * NZ, LANES), F32)
    big = [spin.reshape(3, 2 * NZ, LANES), region.reshape(2 * NZ, LANES), material.reshape(2 * NZ, LANES)]
    spec = demag_spectrum.reshape(6, ROWS, LY)

    def room(x):
        return pltpu.VMEM(x.shape, x.dtype)

    rate, demag = pl.pallas_call(
        kernel,
        out_shape=(out, out),
        in_specs=[hbm] * 3 + [smem] * 4 + [hbm] * (1 + len(tables)),
        out_specs=(vmem, vmem),
        scratch_shapes=[room(x) for x in big + [spec] + tables]
        + [
            pltpu.VMEM((SLOTS, 1536), F32),
            pltpu.VMEM((64, 1536), F32),
        ]
        + [pltpu.VMEM((3, 8, ROWS, 256), F32)] * 4
        + [pltpu.VMEM((64, 1536), F32)] * 2
        + [
            pltpu.VMEM((6, 512, LANES), F32),
            pltpu.VMEM((512, 256), F32),
            pltpu.VMEM((3, 512, 256), F32),
            pltpu.VMEM((3, 2, NZ, LANES), F32),
            pltpu.VMEM((2, NZ, LANES), F32),
            pltpu.VMEM((3, 2, NZ, LANES), F32),
            pltpu.VMEM((2, 3 * NZ, LANES), F32),
            pltpu.VMEM((2, 3 * NZ, LANES), F32),
            pltpu.VMEM((2, 2 * NZ, LANES), F32),
            pltpu.VMEM((2, 2 * NZ, LANES), F32),
            pltpu.VMEM((16, 1536), F32),
            pltpu.VMEM((6, ROWS, 256), F32),
        ]
        + [dma((8,))]
        + [dma((3,))] * 8
        + [dma((4,)), dma((4,))],
        compiler_params=pltpu.CompilerParams(
            collective_id=0, has_side_effects=True, vmem_limit_bytes=56 * 2**20
        ),
    )(*big, saturation, anisotropy, damping, applied, spec, *tables)
    return rate.reshape(3, NZ, 2, LANES), demag.reshape(3, NZ, 2, LANES)


def solution(mesh):
    placed = (
        P(None, None, "wide", "narrow"),
        P(None, "wide", "narrow"),
        P(None, "wide", "narrow"),
        P(),
        P(),
        P(),
        P(),
        P(None, "wide", "narrow", None),
    )
    return jax.shard_map(
        shards,
        mesh=mesh,
        in_specs=placed,
        out_specs=(P(None, None, "wide", "narrow"), P(None, None, "wide", "narrow")),
        check_vma=False,
    )
```

```python
import functools
import math

import jax
import jax.numpy as jnp
import ml_dtypes
import numpy as np
from jax import lax
from jax.experimental import pallas as pl
from jax.experimental.pallas import tpu as pltpu
from jax.sharding import PartitionSpec as P

EXCHANGE = 0.3
MESH = pl.DeviceIdType.MESH
WIDE, NARROW = 64, 8
NZ, LZ, NX, LX, NY, LY = 32, 64, 128, 256, 1024, 2048
SLOTS = 32
ROWS = 32
K = 16
LANES = 128
UNROLL = 9
S1_CHUNKS = ((0, 1), (2,))
S4_CHUNKS = ((0,), (1, 2))
F32, BF16 = jnp.float32, jnp.bfloat16
ROWS_OF = ((0, 3, 4), (3, 1, 5), (4, 5, 2))


def halves(x):
    hi = x.astype(np.float32).astype(ml_dtypes.bfloat16)
    lo = (x - hi.astype(np.float64)).astype(ml_dtypes.bfloat16)
    return np.stack([hi, lo])


def z_parts():
    s, z = np.arange(SLOTS)[:, None], np.arange(NZ)[None]
    angle = 2 * np.pi * (s * z % LZ) / LZ
    re = np.cos(angle)
    im = np.where(s == 0, np.where(z % 2, -1.0, 1.0), -np.sin(angle))
    return re, im


def z_forward():
    return np.concatenate(z_parts(), 0)


def z_inverse():
    re, im = z_parts()
    return np.concatenate([re, re, im, im], 0).T


def complex_matrix(angle):
    c, s = np.cos(angle), np.sin(angle)
    return np.block([[c, -s], [s, c]])


def x_angle():
    x = np.arange(NX).reshape(WIDE, 2).T.reshape(-1)
    return 2 * np.pi * (np.arange(NX)[:, None] * x[None] % LX) / LX


def y_angle():
    p = np.arange(LANES)
    return 2 * np.pi * (p[:, None] * p[None] % LANES) / LANES


def square_tables():
    angle = x_angle()
    tables = [
        complex_matrix(-angle),
        complex_matrix(angle.T) * (2.0 / (LZ * LX * LY)),
        complex_matrix(-y_angle()).T,
        complex_matrix(y_angle()).T,
    ]
    return np.stack([halves(t) for t in tables])


def y_twist():
    k, p = np.arange(K)[:, None], np.arange(LANES)[None]
    angle = 2 * np.pi * (k * p) / LY
    return np.stack([np.cos(angle), -np.sin(angle)]).astype(np.float32)


def mm(a, b):
    dot = functools.partial(jnp.dot, preferred_element_type=F32)
    return dot(a[0], b[0]) + (dot(a[0], b[1]) + dot(a[1], b[0]))


def split(x):
    hi = x.astype(BF16)
    return hi, (x - hi.astype(F32)).astype(BF16)


def turn(v, angle):
    c, s = math.cos(angle), math.sin(angle)
    re, im = v
    if abs(s) < 1e-9 and c > 0:
        return v
    if abs(c) < 1e-9:
        return (-im, re) if s > 0 else (im, -re)
    if abs(c - s) < 1e-9:
        return ((re - im) * c, (re + im) * c)
    if abs(c + s) < 1e-9:
        return ((re + im) * c, (im - re) * c)
    return (re * c - im * s, re * s + im * c)


def fft(values, direction):
    n = len(values)
    if n == 1:
        return values
    even = fft(values[0::2], direction)
    odd = fft(values[1::2], direction)
    odd = [turn(o, direction * 2 * math.pi * k / n) for k, o in enumerate(odd)]
    return ([(e[0] + o[0], e[1] + o[1]) for e, o in zip(even, odd)]
            + [(e[0] - o[0], e[1] - o[1]) for e, o in zip(even, odd)])


def shifted(x, step):
    zero = jnp.zeros((1, x.shape[1]), x.dtype)
    if step > 0:
        return jnp.concatenate([x[1:], zero], 0)
    return jnp.concatenate([zero, x[:-1]], 0)


def cross(x, y):
    return [x[1] * y[2] - x[2] * y[1], x[2] * y[0] - x[0] * y[2], x[0] * y[1] - x[1] * y[0]]


def pick(mat, table):
    out = jnp.full(mat.shape, table[3], F32)
    for i in range(3):
        out = jnp.where(mat == i, table[i], out)
    return out


def other_bit(bit, slot):
    return lax.rem(bit + slot, 2)


def kernel(spin_hbm, region_hbm, material_hbm, satur, aniso, damp, applied, spec_hbm,
           zf_hbm, zi_hbm, square_hbm, twist_hbm,
           rate_out, demag_out,
           spin, region, material, spec, zf, zi, square, twist,
           s1, r1, s2, r2, s3, r3, s4, r4, tensor, work, spectra, direction, satcell, base,
           hx_send, hx, hy_send, hy, spare_row, spare,
           load, send1, recv1, send2, recv2, send3, recv3, send4, recv4, hsend, hrecv):
    w, n = lax.axis_index("wide"), lax.axis_index("narrow")
    half, column = n // 4, lax.rem(n, 4)
    slot = lax.rem(w, SLOTS)
    part = other_bit(w // SLOTS, slot)
    special = slot == 0
    y_device = w <= SLOTS

    loads = [pltpu.make_async_copy(a, b, load.at[i]) for i, (a, b) in enumerate((
        (spin_hbm, spin), (region_hbm, region), (material_hbm, material), (zf_hbm, zf),
        (spec_hbm, spec), (square_hbm, square), (twist_hbm, twist), (zi_hbm, zi)))]
    for copy in loads:
        copy.start()

    def spectrum_device(i):
        return (lax.rem(i, SLOTS) + SLOTS * other_bit(half, i), 4 * (i // SLOTS) + column)

    def brick_device(i):
        return (i, 4 * part + column)

    def is_me(device):
        return (device[0] == w) & (device[1] == n)

    def line_device(i):
        return (jnp.where(i >= 4, SLOTS, slot), 4 * half + lax.rem(i, 4))

    def plane_device(i):
        return (slot + SLOTS * other_bit(i // 4, slot), 4 * half + lax.rem(i, 4))

    barrier = pltpu.get_barrier_semaphore()

    def signal(device):
        pl.semaphore_signal(barrier, inc=1, device_id=device, device_id_type=MESH)

    def greet(device):
        @pl.when(jnp.logical_not(is_me(device)))
        def _():
            signal(device)

    def greet_all(count, device):
        def go(i, carry):
            greet(device(i))
            return carry
        lax.fori_loop(0, count, go, 0)

    on_both = half == part

    def greet_brick(i, carry):
        signal(brick_device(lax.rem(w + i, WIDE)))
        return carry

    @pl.when(jnp.logical_not(on_both))
    def _():
        signal(brick_device(w))
    lax.fori_loop(1, WIDE, greet_brick, 0, unroll=UNROLL)

    def greet_spectrum(i, carry):
        signal(spectrum_device(SLOTS * (1 - part) + i))
        return carry
    lax.fori_loop(0, SLOTS, greet_spectrum, 0, unroll=8)
    greet_all(jnp.where(special, 8, 4), line_device)

    @pl.when(y_device)
    def _():
        greet_all(8, plane_device)

    sides = [(lax.rem(w + 1, WIDE), n), (lax.rem(w + WIDE - 1, WIDE), n),
             (w, lax.rem(n + 1, NARROW)), (w, lax.rem(n + NARROW - 1, NARROW))]
    for device in sides:
        greet(device)
    expected = (96 - jnp.where(on_both, 1, 0)
                + jnp.where(special, 8, 4) - jnp.where(w <= SLOTS, 1, 0)
                + jnp.where(y_device, 7, 0) + 4)

    for copy in loads[:4]:
        copy.wait()
    for xx in range(2):
        rows = pl.ds(xx, NZ, stride=2)
        mag = region[rows, :].astype(F32)
        satcell[xx] = pick(material[rows, :], satur)
        for c in range(3):
            direction[c, xx] = spin[c, rows, :] * mag
    for c in range(3):
        moment = jnp.concatenate([direction[c, xx] * satcell[xx] for xx in range(2)], 1)
        out = mm((zf[0], zf[1]), split(moment))
        s1[:, 512 * c:512 * c + 256] = out[:SLOTS]
        s1[:, 512 * c + 256:512 * c + 512] = out[SLOTS:]

    pl.semaphore_wait(barrier, expected)

    def local(src, dst, sem):
        return pltpu.make_async_copy(src, dst, sem)

    def put(src, dst, dump, send, recv, device):
        @pl.when(is_me(device))
        def _():
            local(src, dst, recv).start()
            local(src, dump, send).start()

        @pl.when(jnp.logical_not(is_me(device)))
        def _():
            pltpu.make_async_remote_copy(
                src, dst, send, recv, device_id=device, device_id_type=MESH).start()

    def done(ref, sem):
        local(ref, ref, sem).wait()


    def columns(chunk):
        return pl.ds(512 * chunk[0], 512 * len(chunk))

    def scatter(count, first, src_row, src, dst, dst_row, dump, cols, send, recv, device):
        def copy(i):
            return pltpu.make_async_remote_copy(
                src.at[pl.ds(src_row(i), 1), cols], dst.at[pl.ds(dst_row, 1), cols], send, recv,
                device_id=device(i), device_id_type=MESH)

        def go(step, carry):
            copy(lax.rem(first + step, count)).start()
            return carry

        lax.fori_loop(1, count, go, 0, unroll=UNROLL)

        @pl.when(on_both)
        def _():
            own = src.at[pl.ds(src_row(first), 1), cols]
            local(own, dst.at[pl.ds(dst_row, 1), cols], recv).start()
            local(own, spare_row.at[pl.ds(dump, 1), cols], send).start()

        @pl.when(jnp.logical_not(on_both))
        def _():
            copy(first).start()

    def spectra_start(g, chunk):
        scatter(64, SLOTS * half + slot, lambda i: lax.rem(i, SLOTS), s1, r1, w, 0, columns(chunk),
                send1.at[g], recv1.at[g], spectrum_device)

    def bricks_start(g, chunk):
        scatter(64, w, lambda i: i, s4, r4, SLOTS * half + slot, 8, columns(chunk),
                send4.at[g], recv4.at[g], brick_device)

    def lines_start(c):
        def go(i, carry):
            put(s2.at[c, i], r2.at[c, 4 * part + column], spare.at[c], send2.at[c], recv2.at[c], line_device(i))
            return carry
        lax.fori_loop(0, jnp.where(special, 8, 4), go, 0)

    def planes_start(c):
        def go(i, carry):
            put(s3.at[c, i], r3.at[c, column + jnp.where(w == SLOTS, 4, 0)], spare.at[3 + c],
                send3.at[c], recv3.at[c], plane_device(i))
            return carry
        lax.fori_loop(0, 8, go, 0)

    def done_blocks(ref, sem):
        @pl.when(special)
        def _():
            done(ref, sem)

        @pl.when(jnp.logical_not(special))
        def _():
            done(ref.at[pl.ds(0, 4)], sem)

    halo = [pltpu.make_async_remote_copy(
        src, dst, hsend.at[i], hrecv.at[i], device_id=sides[i], device_id_type=MESH)
        for i, (src, dst) in enumerate((
            (hx_send.at[0], hx.at[0]), (hx_send.at[1], hx.at[1]),
            (hy_send.at[0], hy.at[0]), (hy_send.at[1], hy.at[1])))]

    for g, chunk in enumerate(S1_CHUNKS):
        spectra_start(g, chunk)
    lane = lax.broadcasted_iota(jnp.int32, (NZ, LANES), 1)
    for xx in range(2):
        for c in range(3):
            hx_send[1 - xx, NZ * c:NZ * c + NZ, :] = direction[c, xx]
        for side, at in ((0, LANES - 1), (1, 0)):
            cols = [jnp.broadcast_to(direction[c, xx][:, at:at + 1], (NZ, LANES)) for c in range(3)]
            hy_send[side, NZ * xx:NZ * xx + NZ, :] = jnp.where(
                lane == 0, cols[0], jnp.where(lane == 1, cols[1], cols[2]))

    for copy in loads[4:]:
        copy.wait()

    @pl.when(y_device)
    def _():
        flat = spec[...].reshape(6 * ROWS, LY)

        def reorder(k, carry):
            ky = lax.broadcasted_iota(jnp.int32, (LY, LANES), 0)
            col = lax.broadcasted_iota(jnp.int32, (LY, LANES), 1)
            choose = jnp.where(ky == K * col + k, 1.0, 0.0).astype(BF16)
            got = jnp.dot(flat, choose, preferred_element_type=F32)
            for g in range(6):
                for t in range(4):
                    tensor[g, pl.ds(pl.multiple_of(128 * t + 8 * k, 8), 8), :] = (
                        got[ROWS * g + 8 * t:ROWS * g + 8 * t + 8])
            return carry

        lax.fori_loop(0, K, reorder, 0)

    flip = jnp.where(half == 1, -1.0, 1.0).astype(F32)

    def x_forward(c):
        got = r1[:, 512 * c:512 * c + 512]
        re = jnp.concatenate([got[:, 0:128], got[:, 128:256] * flip], 0)
        im = jnp.concatenate([got[:, 256:384], got[:, 384:512] * flip], 0)
        rhs = jnp.concatenate([re, jnp.where(special, jnp.zeros_like(im), im)], 0)

        def store(out, at):
            for i in range(4):
                s2[c, at + i, :, 0:128] = out[ROWS * i:ROWS * i + ROWS]
                s2[c, at + i, :, 128:256] = out[128 + ROWS * i:128 + ROWS * i + ROWS]

        store(mm((square[0, 0], square[0, 1]), split(rhs)), 0)

        @pl.when(special)
        def _():
            other = jnp.concatenate([im, jnp.zeros_like(im)], 0)
            store(mm((square[0, 0], square[0, 1]), split(other)), 4)

        lines_start(c)

    def y_forward(c):
        done(r2.at[c], recv2.at[c])

        def go(t, carry):
            rows = pl.ds(pl.multiple_of(8 * t, 8), 8)
            v = [(r2[c, b, rows, 0:128], r2[c, b, rows, 128:256]) for b in range(8)]
            even = fft(v, -1)
            odd = fft([turn(x, -2 * math.pi * b / K) for b, x in enumerate(v)], -1)
            for k in range(K):
                re, im = even[k // 2] if k % 2 == 0 else odd[k // 2]
                cos, sin = twist[0, k:k + 1, :], twist[1, k:k + 1, :]
                at = pl.ds(pl.multiple_of(128 * t + 8 * k, 8), 8)
                work[at, 0:128] = re * cos - im * sin
                work[at, 128:256] = re * sin + im * cos
            return carry

        lax.fori_loop(0, 4, go, 0, unroll=2)

        def multiply(t, carry):
            rows = pl.ds(pl.multiple_of(256 * t, 256), 256)
            spectra[c, rows, :] = mm(split(work[rows, :]), (square[2, 0], square[2, 1]))
            return carry

        lax.fori_loop(0, 2, multiply, 0, unroll=True)

    def ahead(chunk):
        @pl.when(y_device)
        def _():
            for c in chunk:
                y_forward(c)

    for g, chunk in enumerate(S1_CHUNKS):
        done(r1.at[:, columns(chunk)], recv1.at[g])
        for c in chunk:
            x_forward(c)
        if g:
            ahead(S1_CHUNKS[g - 1])
    for copy in halo:
        copy.start()
    ahead(S1_CHUNKS[-1])

    def y_inverse(c):
        a, b, d = ROWS_OF[c]

        def multiply(t, carry):
            rows = pl.ds(pl.multiple_of(256 * t, 256), 256)
            field = [-(tensor[a, rows, :] * spectra[0, rows, at:at + 128]
                       + tensor[b, rows, :] * spectra[1, rows, at:at + 128]
                       + tensor[d, rows, :] * spectra[2, rows, at:at + 128]) for at in (0, 128)]
            work[rows, :] = mm(split(jnp.concatenate(field, 1)), (square[3, 0], square[3, 1]))
            return carry

        lax.fori_loop(0, 2, multiply, 0, unroll=True)

        def go(t, carry):
            u = []
            for k in range(K):
                at = pl.ds(pl.multiple_of(128 * t + 8 * k, 8), 8)
                re, im = work[at, 0:128], work[at, 128:256]
                cos, sin = twist[0, k:k + 1, :], twist[1, k:k + 1, :]
                u.append((re * cos + im * sin, im * cos - re * sin))
            even = fft(u[0::2], 1)
            odd = fft(u[1::2], 1)
            rows = pl.ds(pl.multiple_of(8 * t, 8), 8)
            for j in range(8):
                o = turn(odd[j], 2 * math.pi * j / K)
                s3[c, j, rows, 0:128] = even[j][0] + o[0]
                s3[c, j, rows, 128:256] = even[j][1] + o[1]
            return carry

        lax.fori_loop(0, 4, go, 0, unroll=2)
        planes_start(c)

    def x_inverse(c):
        done_blocks(r3.at[c], recv3.at[c])

        def transform(at):
            got = r3[c, at:at + 4].reshape(4 * ROWS, 256)
            rhs = jnp.concatenate([got[:, 0:128], got[:, 128:256]], 0)
            return mm((square[1, 0], square[1, 1]), split(rhs))

        def store(out, at):
            at += 512 * c
            s4[:, at:at + 128] = out[:WIDE]
            s4[:, at + 128:at + 256] = out[WIDE:] * flip

        out = transform(0) * jnp.where(special, 0.5, 1.0).astype(F32)
        store(out[:NX], 0)

        @pl.when(jnp.logical_not(special))
        def _():
            store(out[NX:], 256)

        @pl.when(special)
        def _():
            store(transform(4)[:NX] * 0.5, 256)

        for g, chunk in enumerate(S4_CHUNKS):
            if c == chunk[-1]:
                bricks_start(g, chunk)

    @pl.when(y_device)
    def _():
        for c in range(3):
            y_inverse(c)

    x_inverse(0)
    x_inverse(1)
    x_inverse(2)

    for copy in halo:
        copy.wait()
    inside = [jnp.where(w > 0, 1.0, 0.0), jnp.where(w < WIDE - 1, 1.0, 0.0),
              jnp.where(n > 0, 1.0, 0.0), jnp.where(n < NARROW - 1, 1.0, 0.0)]
    for xx in range(2):
        total = [jnp.zeros((NZ, LANES), F32)] * 3
        weight = jnp.zeros((NZ, LANES), F32)
        here = [direction[c, xx] for c in range(3)]
        sat = satcell[xx]

        def x_halo(side):
            return [hx[side, NZ * c:NZ * c + NZ, :] * inside[side] for c in range(3)]

        def y_edge(side, c):
            edge = hy[side, NZ * xx:NZ * xx + NZ, c:c + 1] * inside[2 + side]
            return jnp.broadcast_to(edge, (NZ, LANES))

        neighbours = [
            [shifted(d, 1) for d in here],
            [shifted(d, -1) for d in here],
            [direction[c, 0] for c in range(3)] if xx == 1 else x_halo(0),
            [direction[c, 1] for c in range(3)] if xx == 0 else x_halo(1),
            [jnp.where(lane == LANES - 1, y_edge(1, c), pltpu.roll(here[c], LANES - 1, 1)) for c in range(3)],
            [jnp.where(lane == 0, y_edge(0, c), pltpu.roll(here[c], 1, 1)) for c in range(3)],
        ]
        for near in neighbours:
            total = [a + b for a, b in zip(total, near)]
            weight = weight + (near[0] * near[0] + near[1] * near[1] + near[2] * near[2])
        anis = pick(material[pl.ds(xx, NZ, stride=2), :], aniso)
        for c in range(3):
            field = EXCHANGE * (total[c] - weight * here[c]) / sat + applied[c]
            if c == 2:
                field = field + 2.0 * anis / sat * here[2]
            base[c, xx] = field

    for c in range(3):
        for g, chunk in enumerate(S4_CHUNKS):
            if c == chunk[0]:
                done(r4.at[:, columns(chunk)], recv4.at[g])
        got = r4[:, 512 * c:512 * c + 512]
        rhs = jnp.concatenate([got[:, 0:256], got[:, 256:512]], 0)
        out = mm((zi[0], zi[1]), split(rhs))
        for xx in range(2):
            h = out[:, LANES * xx:LANES * xx + LANES]
            demag_out[c, pl.ds(xx, NZ, stride=2), :] = h
            base[c, xx] = base[c, xx] + h
    for xx in range(2):
        rows = pl.ds(xx, NZ, stride=2)
        a = pick(material[rows, :], damp)
        d = [direction[c, xx] for c in range(3)]
        torque = cross(d, [base[c, xx] for c in range(3)])
        second = cross(d, torque)
        for c in range(3):
            rate_out[c, rows, :] = -(torque[c] + a * second[c]) / (1.0 + a * a)

    for g, chunk in enumerate(S1_CHUNKS):
        done(r1.at[:, columns(chunk)], send1.at[g])
    for g, chunk in enumerate(S4_CHUNKS):
        done(s4.at[:, columns(chunk)], send4.at[g])
    for c in range(3):
        done_blocks(s2.at[c], send2.at[c])

    @pl.when(y_device)
    def _():
        for c in range(3):
            done(s3.at[c], send3.at[c])


def shards(spin, region, material, saturation, anisotropy, damping, applied, demag_spectrum):
    vmem = pl.BlockSpec(memory_space=pltpu.VMEM)
    smem = pl.BlockSpec(memory_space=pltpu.SMEM)
    hbm = pl.BlockSpec(memory_space=pltpu.HBM)
    tables = [jnp.asarray(t) for t in (halves(z_forward()), halves(z_inverse()), square_tables(), y_twist())]
    dma = pltpu.SemaphoreType.DMA
    out = jax.ShapeDtypeStruct((3, 2 * NZ, LANES), F32)
    big = [spin.reshape(3, 2 * NZ, LANES), region.reshape(2 * NZ, LANES), material.reshape(2 * NZ, LANES)]
    spec = demag_spectrum.reshape(6, ROWS, LY)

    def room(x):
        return pltpu.VMEM(x.shape, x.dtype)

    rate, demag = pl.pallas_call(
        kernel,
        out_shape=(out, out),
        in_specs=[hbm] * 3 + [smem] * 4 + [hbm] * (1 + len(tables)),
        out_specs=(vmem, vmem),
        scratch_shapes=[room(x) for x in big + [spec] + tables]
        + [
            pltpu.VMEM((SLOTS, 1536), F32),
            pltpu.VMEM((64, 1536), F32),
        ]
        + [pltpu.VMEM((3, 8, ROWS, 256), F32)] * 4
        + [pltpu.VMEM((64, 1536), F32)] * 2
        + [
            pltpu.VMEM((6, 512, LANES), F32),
            pltpu.VMEM((512, 256), F32),
            pltpu.VMEM((3, 512, 256), F32),
            pltpu.VMEM((3, 2, NZ, LANES), F32),
            pltpu.VMEM((2, NZ, LANES), F32),
            pltpu.VMEM((3, 2, NZ, LANES), F32),
            pltpu.VMEM((2, 3 * NZ, LANES), F32),
            pltpu.VMEM((2, 3 * NZ, LANES), F32),
            pltpu.VMEM((2, 2 * NZ, LANES), F32),
            pltpu.VMEM((2, 2 * NZ, LANES), F32),
            pltpu.VMEM((16, 1536), F32),
            pltpu.VMEM((6, ROWS, 256), F32),
        ]
        + [dma((8,))]
        + [dma((3,))] * 8
        + [dma((4,)), dma((4,))],
        compiler_params=pltpu.CompilerParams(
            collective_id=0, has_side_effects=True, vmem_limit_bytes=56 * 2**20
        ),
    )(*big, saturation, anisotropy, damping, applied, spec, *tables)
    return rate.reshape(3, NZ, 2, LANES), demag.reshape(3, NZ, 2, LANES)


def solution(mesh):
    placed = (
        P(None, None, "wide", "narrow"),
        P(None, "wide", "narrow"),
        P(None, "wide", "narrow"),
        P(),
        P(),
        P(),
        P(),
        P(None, "wide", "narrow", None),
    )
    return jax.shard_map(
        shards,
        mesh=mesh,
        in_specs=placed,
        out_specs=(P(None, None, "wide", "narrow"), P(None, None, "wide", "narrow")),
        check_vma=False,
    )
```

```python
import functools
import math

import jax
import jax.numpy as jnp
import ml_dtypes
import numpy as np
from jax import lax
from jax.experimental import pallas as pl
from jax.experimental.pallas import tpu as pltpu
from jax.sharding import PartitionSpec as P

EXCHANGE = 0.3
MESH = pl.DeviceIdType.MESH
WIDE, NARROW = 64, 8
NZ, LZ, NX, LX, NY, LY = 32, 64, 128, 256, 1024, 2048
SLOTS = 32
ROWS = 32
K = 16
LANES = 128
UNROLL = 9
S1_CHUNKS = ((0, 1), (2,))
S4_CHUNKS = ((0,), (1, 2))
F32, BF16 = jnp.float32, jnp.bfloat16
ROWS_OF = ((0, 3, 4), (3, 1, 5), (4, 5, 2))


def halves(x):
    hi = x.astype(np.float32).astype(ml_dtypes.bfloat16)
    lo = (x - hi.astype(np.float64)).astype(ml_dtypes.bfloat16)
    return np.stack([hi, lo])


def z_parts():
    s, z = np.arange(SLOTS)[:, None], np.arange(NZ)[None]
    angle = 2 * np.pi * (s * z % LZ) / LZ
    re = np.cos(angle)
    im = np.where(s == 0, np.where(z % 2, -1.0, 1.0), -np.sin(angle))
    return re, im


def z_forward():
    return np.concatenate(z_parts(), 0)


def z_inverse():
    re, im = z_parts()
    return np.concatenate([re, re, im, im], 0).T


def complex_matrix(angle):
    c, s = np.cos(angle), np.sin(angle)
    return np.block([[c, -s], [s, c]])


def x_angle():
    x = np.arange(NX).reshape(WIDE, 2).T.reshape(-1)
    return 2 * np.pi * (np.arange(NX)[:, None] * x[None] % LX) / LX


def y_angle():
    p = np.arange(LANES)
    return 2 * np.pi * (p[:, None] * p[None] % LANES) / LANES


def square_tables():
    angle = x_angle()
    tables = [
        complex_matrix(-angle),
        complex_matrix(angle.T) * (2.0 / (LZ * LX * LY)),
        complex_matrix(-y_angle()).T,
        complex_matrix(y_angle()).T,
    ]
    return np.stack([halves(t) for t in tables])


def y_twist():
    k, p = np.arange(K)[:, None], np.arange(LANES)[None]
    angle = 2 * np.pi * (k * p) / LY
    return np.stack([np.cos(angle), -np.sin(angle)]).astype(np.float32)


def mm(a, b):
    dot = functools.partial(jnp.dot, preferred_element_type=F32)
    return dot(a[0], b[0]) + (dot(a[0], b[1]) + dot(a[1], b[0]))


def split(x):
    hi = x.astype(BF16)
    return hi, (x - hi.astype(F32)).astype(BF16)


def turn(v, angle):
    c, s = math.cos(angle), math.sin(angle)
    re, im = v
    if abs(s) < 1e-9 and c > 0:
        return v
    if abs(c) < 1e-9:
        return (-im, re) if s > 0 else (im, -re)
    if abs(c - s) < 1e-9:
        return ((re - im) * c, (re + im) * c)
    if abs(c + s) < 1e-9:
        return ((re + im) * c, (im - re) * c)
    return (re * c - im * s, re * s + im * c)


def fft(values, direction):
    n = len(values)
    if n == 1:
        return values
    even = fft(values[0::2], direction)
    odd = fft(values[1::2], direction)
    odd = [turn(o, direction * 2 * math.pi * k / n) for k, o in enumerate(odd)]
    return ([(e[0] + o[0], e[1] + o[1]) for e, o in zip(even, odd)]
            + [(e[0] - o[0], e[1] - o[1]) for e, o in zip(even, odd)])


def shifted(x, step):
    zero = jnp.zeros((1, x.shape[1]), x.dtype)
    if step > 0:
        return jnp.concatenate([x[1:], zero], 0)
    return jnp.concatenate([zero, x[:-1]], 0)


def cross(x, y):
    return [x[1] * y[2] - x[2] * y[1], x[2] * y[0] - x[0] * y[2], x[0] * y[1] - x[1] * y[0]]


def pick(mat, table):
    out = jnp.full(mat.shape, table[3], F32)
    for i in range(3):
        out = jnp.where(mat == i, table[i], out)
    return out


def other_bit(bit, slot):
    return lax.rem(bit + slot, 2)


def kernel(spin_hbm, region_hbm, material_hbm, satur, aniso, damp, applied, spec_hbm,
           zf_hbm, zi_hbm, square_hbm, twist_hbm,
           rate_out, demag_out,
           spin, region, material, spec, zf, zi, square, twist,
           s1, r1, s2, r2, s3, r3, s4, r4, tensor, work, spectra, direction, satcell, base,
           hx_send, hx, hy_send, hy, spare_row, spare,
           load, send1, recv1, send2, recv2, send3, recv3, send4, recv4, hsend, hrecv):
    w, n = lax.axis_index("wide"), lax.axis_index("narrow")
    half, column = n // 4, lax.rem(n, 4)
    slot = lax.rem(w, SLOTS)
    part = other_bit(w // SLOTS, slot)
    special = slot == 0
    y_device = w <= SLOTS

    loads = [pltpu.make_async_copy(a, b, load.at[i]) for i, (a, b) in enumerate((
        (spin_hbm, spin), (region_hbm, region), (material_hbm, material), (zf_hbm, zf),
        (spec_hbm, spec), (square_hbm, square), (twist_hbm, twist), (zi_hbm, zi)))]
    for copy in loads[:4]:
        copy.start()

    def spectrum_device(i):
        return (lax.rem(i, SLOTS) + SLOTS * other_bit(half, i), 4 * (i // SLOTS) + column)

    def brick_device(i):
        return (i, 4 * part + column)

    def is_me(device):
        return (device[0] == w) & (device[1] == n)

    def line_device(i):
        return (jnp.where(i >= 4, SLOTS, slot), 4 * half + lax.rem(i, 4))

    def plane_device(i):
        return (slot + SLOTS * other_bit(i // 4, slot), 4 * half + lax.rem(i, 4))

    barrier = pltpu.get_barrier_semaphore()

    def signal(device):
        pl.semaphore_signal(barrier, inc=1, device_id=device, device_id_type=MESH)

    def greet(device):
        @pl.when(jnp.logical_not(is_me(device)))
        def _():
            signal(device)

    def greet_all(count, device):
        def go(i, carry):
            greet(device(i))
            return carry
        lax.fori_loop(0, count, go, 0)

    on_both = half == part

    def greet_brick(i, carry):
        signal(brick_device(lax.rem(w + i, WIDE)))
        return carry

    @pl.when(jnp.logical_not(on_both))
    def _():
        signal(brick_device(w))
    lax.fori_loop(1, WIDE, greet_brick, 0, unroll=UNROLL)

    def greet_spectrum(i, carry):
        signal(spectrum_device(SLOTS * (1 - part) + i))
        return carry
    lax.fori_loop(0, SLOTS, greet_spectrum, 0, unroll=8)
    greet_all(jnp.where(special, 8, 4), line_device)

    @pl.when(y_device)
    def _():
        greet_all(8, plane_device)

    sides = [(lax.rem(w + 1, WIDE), n), (lax.rem(w + WIDE - 1, WIDE), n),
             (w, lax.rem(n + 1, NARROW)), (w, lax.rem(n + NARROW - 1, NARROW))]
    for device in sides:
        greet(device)
    expected = (96 - jnp.where(on_both, 1, 0)
                + jnp.where(special, 8, 4) - jnp.where(w <= SLOTS, 1, 0)
                + jnp.where(y_device, 7, 0) + 4)

    for copy in loads[:4]:
        copy.wait()
    for xx in range(2):
        rows = pl.ds(xx, NZ, stride=2)
        mag = region[rows, :].astype(F32)
        satcell[xx] = pick(material[rows, :], satur)
        for c in range(3):
            direction[c, xx] = spin[c, rows, :] * mag
    def z_forward_part(c):
        moment = jnp.concatenate([direction[c, xx] * satcell[xx] for xx in range(2)], 1)
        out = mm((zf[0], zf[1]), split(moment))
        s1[:, 512 * c:512 * c + 256] = out[:SLOTS]
        s1[:, 512 * c + 256:512 * c + 512] = out[SLOTS:]

    for c in S1_CHUNKS[0]:
        z_forward_part(c)

    pl.semaphore_wait(barrier, expected)

    def local(src, dst, sem):
        return pltpu.make_async_copy(src, dst, sem)

    def put(src, dst, dump, send, recv, device):
        @pl.when(is_me(device))
        def _():
            local(src, dst, recv).start()
            local(src, dump, send).start()

        @pl.when(jnp.logical_not(is_me(device)))
        def _():
            pltpu.make_async_remote_copy(
                src, dst, send, recv, device_id=device, device_id_type=MESH).start()

    def done(ref, sem):
        local(ref, ref, sem).wait()


    def columns(chunk):
        return pl.ds(512 * chunk[0], 512 * len(chunk))

    def scatter(count, first, src_row, src, dst, dst_row, dump, cols, send, recv, device):
        def copy(i):
            return pltpu.make_async_remote_copy(
                src.at[pl.ds(src_row(i), 1), cols], dst.at[pl.ds(dst_row, 1), cols], send, recv,
                device_id=device(i), device_id_type=MESH)

        def go(step, carry):
            copy(lax.rem(first + step, count)).start()
            return carry

        lax.fori_loop(1, count, go, 0, unroll=UNROLL)

        @pl.when(on_both)
        def _():
            own = src.at[pl.ds(src_row(first), 1), cols]
            local(own, dst.at[pl.ds(dst_row, 1), cols], recv).start()
            local(own, spare_row.at[pl.ds(dump, 1), cols], send).start()

        @pl.when(jnp.logical_not(on_both))
        def _():
            copy(first).start()

    def spectra_start(g, chunk):
        scatter(64, SLOTS * half + slot, lambda i: lax.rem(i, SLOTS), s1, r1, w, 0, columns(chunk),
                send1.at[g], recv1.at[g], spectrum_device)

    def bricks_start(g, chunk):
        scatter(64, w, lambda i: i, s4, r4, SLOTS * half + slot, 8, columns(chunk),
                send4.at[g], recv4.at[g], brick_device)

    def lines_start(c):
        def go(i, carry):
            put(s2.at[c, i], r2.at[c, 4 * part + column], spare.at[c], send2.at[c], recv2.at[c], line_device(i))
            return carry
        lax.fori_loop(0, jnp.where(special, 8, 4), go, 0)

    def planes_start(c):
        def go(i, carry):
            put(s3.at[c, i], r3.at[c, column + jnp.where(w == SLOTS, 4, 0)], spare.at[3 + c],
                send3.at[c], recv3.at[c], plane_device(i))
            return carry
        lax.fori_loop(0, 8, go, 0)

    def done_blocks(ref, sem):
        @pl.when(special)
        def _():
            done(ref, sem)

        @pl.when(jnp.logical_not(special))
        def _():
            done(ref.at[pl.ds(0, 4)], sem)

    halo = [pltpu.make_async_remote_copy(
        src, dst, hsend.at[i], hrecv.at[i], device_id=sides[i], device_id_type=MESH)
        for i, (src, dst) in enumerate((
            (hx_send.at[0], hx.at[0]), (hx_send.at[1], hx.at[1]),
            (hy_send.at[0], hy.at[0]), (hy_send.at[1], hy.at[1])))]

    for g, chunk in enumerate(S1_CHUNKS):
        if g:
            for c in chunk:
                z_forward_part(c)
        spectra_start(g, chunk)
        if g == 0:
            for copy in loads[4:]:
                copy.start()
    lane = lax.broadcasted_iota(jnp.int32, (NZ, LANES), 1)
    for xx in range(2):
        for c in range(3):
            hx_send[1 - xx, NZ * c:NZ * c + NZ, :] = direction[c, xx]
        for side, at in ((0, LANES - 1), (1, 0)):
            cols = [jnp.broadcast_to(direction[c, xx][:, at:at + 1], (NZ, LANES)) for c in range(3)]
            hy_send[side, NZ * xx:NZ * xx + NZ, :] = jnp.where(
                lane == 0, cols[0], jnp.where(lane == 1, cols[1], cols[2]))

    for copy in loads[4:]:
        copy.wait()

    @pl.when(y_device)
    def _():
        flat = spec[...].reshape(6 * ROWS, LY)

        def reorder(k, carry):
            ky = lax.broadcasted_iota(jnp.int32, (LY, LANES), 0)
            col = lax.broadcasted_iota(jnp.int32, (LY, LANES), 1)
            choose = jnp.where(ky == K * col + k, 1.0, 0.0).astype(BF16)
            got = jnp.dot(flat, choose, preferred_element_type=F32)
            for g in range(6):
                for t in range(4):
                    tensor[g, pl.ds(pl.multiple_of(128 * t + 8 * k, 8), 8), :] = (
                        got[ROWS * g + 8 * t:ROWS * g + 8 * t + 8])
            return carry

        lax.fori_loop(0, K, reorder, 0)

    flip = jnp.where(half == 1, -1.0, 1.0).astype(F32)

    def x_forward(c):
        got = r1[:, 512 * c:512 * c + 512]
        re = jnp.concatenate([got[:, 0:128], got[:, 128:256] * flip], 0)
        im = jnp.concatenate([got[:, 256:384], got[:, 384:512] * flip], 0)
        rhs = jnp.concatenate([re, jnp.where(special, jnp.zeros_like(im), im)], 0)

        def store(out, at):
            for i in range(4):
                s2[c, at + i, :, 0:128] = out[ROWS * i:ROWS * i + ROWS]
                s2[c, at + i, :, 128:256] = out[128 + ROWS * i:128 + ROWS * i + ROWS]

        store(mm((square[0, 0], square[0, 1]), split(rhs)), 0)

        @pl.when(special)
        def _():
            other = jnp.concatenate([im, jnp.zeros_like(im)], 0)
            store(mm((square[0, 0], square[0, 1]), split(other)), 4)

        lines_start(c)

    def y_forward(c):
        done(r2.at[c], recv2.at[c])

        def go(t, carry):
            rows = pl.ds(pl.multiple_of(8 * t, 8), 8)
            v = [(r2[c, b, rows, 0:128], r2[c, b, rows, 128:256]) for b in range(8)]
            even = fft(v, -1)
            odd = fft([turn(x, -2 * math.pi * b / K) for b, x in enumerate(v)], -1)
            for k in range(K):
                re, im = even[k // 2] if k % 2 == 0 else odd[k // 2]
                cos, sin = twist[0, k:k + 1, :], twist[1, k:k + 1, :]
                at = pl.ds(pl.multiple_of(128 * t + 8 * k, 8), 8)
                work[at, 0:128] = re * cos - im * sin
                work[at, 128:256] = re * sin + im * cos
            return carry

        lax.fori_loop(0, 4, go, 0, unroll=2)

        def multiply(t, carry):
            rows = pl.ds(pl.multiple_of(256 * t, 256), 256)
            spectra[c, rows, :] = mm(split(work[rows, :]), (square[2, 0], square[2, 1]))
            return carry

        lax.fori_loop(0, 2, multiply, 0, unroll=True)

    def ahead(chunk):
        @pl.when(y_device)
        def _():
            for c in chunk:
                y_forward(c)

    for g, chunk in enumerate(S1_CHUNKS):
        done(r1.at[:, columns(chunk)], recv1.at[g])
        for c in chunk:
            x_forward(c)
        if g:
            ahead(S1_CHUNKS[g - 1])
    for copy in halo:
        copy.start()
    ahead(S1_CHUNKS[-1])

    def y_inverse(c):
        a, b, d = ROWS_OF[c]

        def multiply(t, carry):
            rows = pl.ds(pl.multiple_of(256 * t, 256), 256)
            field = [-(tensor[a, rows, :] * spectra[0, rows, at:at + 128]
                       + tensor[b, rows, :] * spectra[1, rows, at:at + 128]
                       + tensor[d, rows, :] * spectra[2, rows, at:at + 128]) for at in (0, 128)]
            work[rows, :] = mm(split(jnp.concatenate(field, 1)), (square[3, 0], square[3, 1]))
            return carry

        lax.fori_loop(0, 2, multiply, 0, unroll=True)

        def go(t, carry):
            u = []
            for k in range(K):
                at = pl.ds(pl.multiple_of(128 * t + 8 * k, 8), 8)
                re, im = work[at, 0:128], work[at, 128:256]
                cos, sin = twist[0, k:k + 1, :], twist[1, k:k + 1, :]
                u.append((re * cos + im * sin, im * cos - re * sin))
            even = fft(u[0::2], 1)
            odd = fft(u[1::2], 1)
            rows = pl.ds(pl.multiple_of(8 * t, 8), 8)
            for j in range(8):
                o = turn(odd[j], 2 * math.pi * j / K)
                s3[c, j, rows, 0:128] = even[j][0] + o[0]
                s3[c, j, rows, 128:256] = even[j][1] + o[1]
            return carry

        lax.fori_loop(0, 4, go, 0, unroll=2)
        planes_start(c)

    def x_inverse(c):
        done_blocks(r3.at[c], recv3.at[c])

        def transform(at):
            got = r3[c, at:at + 4].reshape(4 * ROWS, 256)
            rhs = jnp.concatenate([got[:, 0:128], got[:, 128:256]], 0)
            return mm((square[1, 0], square[1, 1]), split(rhs))

        def store(out, at):
            at += 512 * c
            s4[:, at:at + 128] = out[:WIDE]
            s4[:, at + 128:at + 256] = out[WIDE:] * flip

        out = transform(0) * jnp.where(special, 0.5, 1.0).astype(F32)
        store(out[:NX], 0)

        @pl.when(jnp.logical_not(special))
        def _():
            store(out[NX:], 256)

        @pl.when(special)
        def _():
            store(transform(4)[:NX] * 0.5, 256)

        for g, chunk in enumerate(S4_CHUNKS):
            if c == chunk[-1]:
                bricks_start(g, chunk)

    @pl.when(y_device)
    def _():
        for c in range(3):
            y_inverse(c)

    x_inverse(0)
    x_inverse(1)
    x_inverse(2)

    for copy in halo:
        copy.wait()
    inside = [jnp.where(w > 0, 1.0, 0.0), jnp.where(w < WIDE - 1, 1.0, 0.0),
              jnp.where(n > 0, 1.0, 0.0), jnp.where(n < NARROW - 1, 1.0, 0.0)]
    for xx in range(2):
        total = [jnp.zeros((NZ, LANES), F32)] * 3
        weight = jnp.zeros((NZ, LANES), F32)
        here = [direction[c, xx] for c in range(3)]
        sat = satcell[xx]

        def x_halo(side):
            return [hx[side, NZ * c:NZ * c + NZ, :] * inside[side] for c in range(3)]

        def y_edge(side, c):
            edge = hy[side, NZ * xx:NZ * xx + NZ, c:c + 1] * inside[2 + side]
            return jnp.broadcast_to(edge, (NZ, LANES))

        neighbours = [
            [shifted(d, 1) for d in here],
            [shifted(d, -1) for d in here],
            [direction[c, 0] for c in range(3)] if xx == 1 else x_halo(0),
            [direction[c, 1] for c in range(3)] if xx == 0 else x_halo(1),
            [jnp.where(lane == LANES - 1, y_edge(1, c), pltpu.roll(here[c], LANES - 1, 1)) for c in range(3)],
            [jnp.where(lane == 0, y_edge(0, c), pltpu.roll(here[c], 1, 1)) for c in range(3)],
        ]
        for near in neighbours:
            total = [a + b for a, b in zip(total, near)]
            weight = weight + (near[0] * near[0] + near[1] * near[1] + near[2] * near[2])
        anis = pick(material[pl.ds(xx, NZ, stride=2), :], aniso)
        for c in range(3):
            field = EXCHANGE * (total[c] - weight * here[c]) / sat + applied[c]
            if c == 2:
                field = field + 2.0 * anis / sat * here[2]
            base[c, xx] = field

    for c in range(3):
        for g, chunk in enumerate(S4_CHUNKS):
            if c == chunk[0]:
                done(r4.at[:, columns(chunk)], recv4.at[g])
        got = r4[:, 512 * c:512 * c + 512]
        rhs = jnp.concatenate([got[:, 0:256], got[:, 256:512]], 0)
        out = mm((zi[0], zi[1]), split(rhs))
        for xx in range(2):
            h = out[:, LANES * xx:LANES * xx + LANES]
            demag_out[c, pl.ds(xx, NZ, stride=2), :] = h
            base[c, xx] = base[c, xx] + h
    for xx in range(2):
        rows = pl.ds(xx, NZ, stride=2)
        a = pick(material[rows, :], damp)
        d = [direction[c, xx] for c in range(3)]
        torque = cross(d, [base[c, xx] for c in range(3)])
        second = cross(d, torque)
        for c in range(3):
            rate_out[c, rows, :] = -(torque[c] + a * second[c]) / (1.0 + a * a)

    for g, chunk in enumerate(S1_CHUNKS):
        done(r1.at[:, columns(chunk)], send1.at[g])
    for g, chunk in enumerate(S4_CHUNKS):
        done(s4.at[:, columns(chunk)], send4.at[g])
    for c in range(3):
        done_blocks(s2.at[c], send2.at[c])

    @pl.when(y_device)
    def _():
        for c in range(3):
            done(s3.at[c], send3.at[c])


def shards(spin, region, material, saturation, anisotropy, damping, applied, demag_spectrum):
    vmem = pl.BlockSpec(memory_space=pltpu.VMEM)
    smem = pl.BlockSpec(memory_space=pltpu.SMEM)
    hbm = pl.BlockSpec(memory_space=pltpu.HBM)
    tables = [jnp.asarray(t) for t in (halves(z_forward()), halves(z_inverse()), square_tables(), y_twist())]
    dma = pltpu.SemaphoreType.DMA
    out = jax.ShapeDtypeStruct((3, 2 * NZ, LANES), F32)
    big = [spin.reshape(3, 2 * NZ, LANES), region.reshape(2 * NZ, LANES), material.reshape(2 * NZ, LANES)]
    spec = demag_spectrum.reshape(6, ROWS, LY)

    def room(x):
        return pltpu.VMEM(x.shape, x.dtype)

    rate, demag = pl.pallas_call(
        kernel,
        out_shape=(out, out),
        in_specs=[hbm] * 3 + [smem] * 4 + [hbm] * (1 + len(tables)),
        out_specs=(vmem, vmem),
        scratch_shapes=[room(x) for x in big + [spec] + tables]
        + [
            pltpu.VMEM((SLOTS, 1536), F32),
            pltpu.VMEM((64, 1536), F32),
        ]
        + [pltpu.VMEM((3, 8, ROWS, 256), F32)] * 4
        + [pltpu.VMEM((64, 1536), F32)] * 2
        + [
            pltpu.VMEM((6, 512, LANES), F32),
            pltpu.VMEM((512, 256), F32),
            pltpu.VMEM((3, 512, 256), F32),
            pltpu.VMEM((3, 2, NZ, LANES), F32),
            pltpu.VMEM((2, NZ, LANES), F32),
            pltpu.VMEM((3, 2, NZ, LANES), F32),
            pltpu.VMEM((2, 3 * NZ, LANES), F32),
            pltpu.VMEM((2, 3 * NZ, LANES), F32),
            pltpu.VMEM((2, 2 * NZ, LANES), F32),
            pltpu.VMEM((2, 2 * NZ, LANES), F32),
            pltpu.VMEM((16, 1536), F32),
            pltpu.VMEM((6, ROWS, 256), F32),
        ]
        + [dma((8,))]
        + [dma((3,))] * 8
        + [dma((4,)), dma((4,))],
        compiler_params=pltpu.CompilerParams(
            collective_id=0, has_side_effects=True, vmem_limit_bytes=56 * 2**20
        ),
    )(*big, saturation, anisotropy, damping, applied, spec, *tables)
    return rate.reshape(3, NZ, 2, LANES), demag.reshape(3, NZ, 2, LANES)


def solution(mesh):
    placed = (
        P(None, None, "wide", "narrow"),
        P(None, "wide", "narrow"),
        P(None, "wide", "narrow"),
        P(),
        P(),
        P(),
        P(),
        P(None, "wide", "narrow", None),
    )
    return jax.shard_map(
        shards,
        mesh=mesh,
        in_specs=placed,
        out_specs=(P(None, None, "wide", "narrow"), P(None, None, "wide", "narrow")),
        check_vma=False,
    )
```
